32 devices in a mesh: sub: 8 (over z, y), grp: 4 (over x, core).
Axes of the slice: x: 2, y: 2, z: 4, core: 2. Of those that a mesh axis runs over, the one named last changes fastest.
Arguments:
- facies: int32 [128, 32, 128], P('sub', 'grp'), may hold values from 0 to 7
- facies_perm: float32 [8], replicated, may hold values from 0.2 to 5
- perm_scale: float32 [128, 32, 128], P('sub', 'grp'), may hold values from 0.5 to 2
- source: float32 [128, 32, 128], P('sub', 'grp'), may hold values from -6 to 6
- pressure_start: float32 [128, 32, 128], P('sub', 'grp'), may hold values from -4 to 4
- intersection_depth: int32 [7], replicated, may hold values from 1 to 4, as said below
Outputs:
- pressure: float32 [128, 32, 128], P('sub', 'grp')
The draws below stay inside these ranges and needn't reach their ends.
Inputs may be any that keep to these rules, and one draw needn't show every extreme that they name: `intersection_depth`: every entry is a margin depth; some entry equals 4 in every draw.
All inputs are finite; a program needn't handle non-finite values.
Results may differ from the reference program's by a relative error of at most 0.0003.
Values sent between devices are 32-bit elements; how exact they have to be, the bound alone decides.
A program may use at most 64 MiB of HBM per device.

```python
import math
import jax
import jax.numpy as jnp
from jax import lax

CZ = 16
NY = 128
OV = 4
BL = 8
ROUNDS = 4
OUTER = 2
FACIES = 8
NZ = 128
NX = 32
PAIRS = 7
N_SUB = 8


def draw_intersection_depth(key, part):
    depths = jax.random.randint(key, (PAIRS,), 1, OV + 1)
    chosen = jax.random.randint(jax.random.fold_in(key, 7), (), 0, PAIRS)
    return jnp.where(jnp.arange(PAIRS) == chosen, OV, depths).astype(jnp.int32)


def touch_ends(array, rng, low, largest):
    index_at = [jax.random.randint(jax.random.fold_in(rng, axis), (), 0, length) for axis, length in enumerate(array.shape)]
    main_axis = array.shape.index(max(array.shape))
    beside = index_at[:main_axis] + [(index_at[main_axis] + 1) % array.shape[main_axis]] + index_at[main_axis + 1:]
    return array.at[tuple(index_at)].set(low).at[tuple(beside)].set(largest)


def level_of(own_key, shape, pieces, low, top_value):
    loudness, own = 1.0, jax.random.fold_in(own_key, 6)
    for dim, shards_of in pieces:
        steps = jnp.exp(jax.random.uniform(jax.random.fold_in(own, dim), (shards_of,), jnp.float32, low / len(pieces), top_value / len(pieces)))
        loudness = loudness * jnp.repeat(steps, shape[dim] // shards_of).reshape([-1 if axis == dim else 1 for axis in range(len(shape))])
    return loudness


def normal_values(key, dims, spread, limit, shards=(), kind=jnp.bfloat16):
    factor_of = level_of(key, dims, shards, -0.22, 0.18) if shards else 1.0
    values = jax.random.normal(key, dims, jnp.float32) * spread * factor_of
    return jnp.minimum(jnp.maximum(values, -limit), limit).astype(kind)


def setup_inputs(seed: int = 0) -> dict:
    key_list = jax.random.split(jax.random.key(seed), 7)
    return {
        "facies": touch_ends(jax.random.randint(key_list[0], (NZ, NX, NY), 0, FACIES), jax.random.fold_in(key_list[0], 1), 0, FACIES - 1).astype(jnp.int32),
        "facies_perm": jnp.clip(jnp.exp(jax.random.uniform(key_list[1], (FACIES,), jnp.float32, math.log(0.2), math.log(5.0))), 0.2, 5.0),
        "perm_scale": jnp.clip(jnp.exp(math.log(2.0) - 1.3862944 * jax.random.uniform(key_list[2], (NZ, NX, NY), jnp.float32) ** level_of(key_list[2], (NZ, NX, NY), ((0, 8), (1, 4)), -0.2, 0.2)), 0.5, 2.0),
        "source": normal_values(key_list[3], (NZ, NX, NY), 1.0, 6.0, ((0, 8), (1, 4)), jnp.float32),
        "pressure_start": normal_values(key_list[4], (NZ, NX, NY), 0.5, 4.0, ((0, 8), (1, 4)), jnp.float32),
        "intersection_depth": draw_intersection_depth(jax.random.fold_in(key_list[6], 71), 0),
    }


STORE = 0.02


def relax_weight(round_index):
    return 1.0 / (1.4 + 0.6 * math.cos(math.pi * (2 * round_index + 1) / (2 * ROUNDS)))


def harmonic(former, second):
    inside = jnp.where((former > 0) & (second > 0), 1.0, 0.0)
    safe_former = jnp.where(former > 0, former, 1.0)
    safe_second = jnp.where(second > 0, second, 1.0)
    return inside * (2.0 * safe_former * safe_second / (safe_former + safe_second))


def neighbours(field, line_axis):
    extent = field.shape[line_axis]
    zero_plane = jnp.zeros_like(lax.slice_in_dim(field, 0, 1, axis=line_axis))
    lower_side = jnp.concatenate([zero_plane, lax.slice_in_dim(field, 0, extent - 1, axis=line_axis)], axis=line_axis)
    upper_side = jnp.concatenate([lax.slice_in_dim(field, 1, extent, axis=line_axis), zero_plane], axis=line_axis)
    return lower_side, upper_side


def apply_operator(coeffs, center, below_rows, above_rows, left_side, right_side):
    diagonal, face_below, face_above, face_left, face_right, face_front, face_back = coeffs
    front_cols, back_cols = neighbours(center, 2)
    coupled = face_below * below_rows + face_above * above_rows + face_left * left_side + face_right * right_side + face_front * front_cols + face_back * back_cols
    return diagonal * center - coupled


def operate(coeffs, field):
    below_rows, above_rows = neighbours(field, 0)
    left_side, right_side = neighbours(field, 1)
    return apply_operator(coeffs, field, below_rows, above_rows, left_side, right_side)


def pack_lines(field, line_axis):
    extents = field.shape
    split_dims = extents[:line_axis] + (extents[line_axis] // BL, BL) + extents[line_axis + 1:]
    return jnp.moveaxis(field.reshape(split_dims), line_axis + 1, 0).reshape(BL, -1)


def unpack_lines(packed, line_axis, extents):
    split_dims = extents[:line_axis] + (extents[line_axis] // BL, BL) + extents[line_axis + 1:]
    moved_dims = (BL,) + split_dims[:line_axis + 1] + split_dims[line_axis + 2:]
    return jnp.moveaxis(packed.reshape(moved_dims), 0, line_axis + 1).reshape(extents)


def factor_lines(lower_band, middle, upper_band):
    pivots = [middle[0]]
    multipliers = [jnp.zeros_like(middle[0])]
    for position in range(1, BL):
        multiplier = lower_band[position] / pivots[position - 1]
        multipliers.append(multiplier)
        pivots.append(middle[position] - multiplier * upper_band[position - 1])
    return jnp.stack(multipliers), 1.0 / jnp.stack(pivots), upper_band


def solve_lines(factors, packed_rhs):
    multipliers, inverse, upper_band = factors
    forward = [packed_rhs[0]]
    for position in range(1, BL):
        forward.append(packed_rhs[position] - multipliers[position] * forward[position - 1])
    result = [None] * BL
    result[BL - 1] = forward[BL - 1] * inverse[BL - 1]
    for position in range(BL - 2, -1, -1):
        result[position] = (forward[position] - upper_band[position] * result[position + 1]) * inverse[position]
    return jnp.stack(result)


def line_factors(coeffs, active, line_axis):
    diagonal = coeffs[0]
    face_low = coeffs[2 * line_axis + 1]
    face_high = coeffs[2 * line_axis + 2]
    extent = diagonal.shape[line_axis]
    broadcast_shape = [1, 1, 1]
    broadcast_shape[line_axis] = extent
    position = (jnp.arange(extent, dtype=jnp.int32) % BL).reshape(broadcast_shape)
    if line_axis == 0:
        active_low, active_high = neighbours(active, 0)
    else:
        active_low = active
        active_high = active
    lower_band = jnp.where(position != 0, -face_low * active * active_low, 0.0)
    upper_band = jnp.where(position != BL - 1, -face_high * active * active_high, 0.0)
    middle = jnp.where(active > 0, diagonal, 1.0)
    return factor_lines(pack_lines(lower_band, line_axis), pack_lines(middle, line_axis), pack_lines(upper_band, line_axis))


def correction_step(factors, line_axis, update, weight_now, estimate):
    solved = solve_lines(factors, pack_lines(update, line_axis))
    return estimate + weight_now * unpack_lines(solved, line_axis, estimate.shape)


def reference(facies, facies_perm, perm_scale, source, pressure_start, intersection_depth):
    permeability = facies_perm[facies] * perm_scale
    padded = jnp.pad(permeability, 1)
    faces_vertical = harmonic(padded[:-1, 1:-1, 1:-1], padded[1:, 1:-1, 1:-1])
    faces_across = harmonic(padded[1:-1, :-1, 1:-1], padded[1:-1, 1:, 1:-1])
    faces_along = harmonic(padded[1:-1, 1:-1, :-1], padded[1:-1, 1:-1, 1:])
    face_below = faces_vertical[:-1]
    face_above = faces_vertical[1:]
    face_left = faces_across[:, :-1]
    face_right = faces_across[:, 1:]
    face_front = faces_along[:, :, :-1]
    face_back = faces_along[:, :, 1:]
    diagonal = STORE + face_below + face_above + face_left + face_right + face_front + face_back
    coeffs = (diagonal, face_below, face_above, face_left, face_right, face_front, face_back)
    margin_rows = CZ + 2 * OV
    padded_coeffs = tuple(jnp.pad(member, ((OV, OV), (0, 0), (0, 0))) for member in coeffs)
    bounds = jnp.concatenate([jnp.zeros((1,), jnp.int32), intersection_depth.astype(jnp.int32), jnp.zeros((1,), jnp.int32)])
    offsets = jnp.arange(margin_rows, dtype=jnp.int32) - OV
    pressure = pressure_start
    for outer_turn in range(OUTER):
        residual = source - operate(coeffs, pressure)
        residual_pad = jnp.pad(residual, ((OV, OV), (0, 0), (0, 0)))

        def one_slab(slab_index, combined):
            start = (slab_index * CZ).astype(jnp.int32)
            local = tuple(lax.dynamic_slice_in_dim(member, start, margin_rows, 0) for member in padded_coeffs)
            target = lax.dynamic_slice_in_dim(residual_pad, start, margin_rows, 0)
            depth_low = bounds[slab_index]
            depth_high = bounds[slab_index + 1]
            inside_slab = (offsets >= -depth_low) & (offsets < CZ + depth_high)
            band_rows = (offsets < depth_low) | (offsets >= CZ - depth_high)
            active = jnp.where(inside_slab, 1.0, 0.0).reshape(margin_rows, 1, 1)
            weight = jnp.where(inside_slab & band_rows, 0.5, jnp.where(inside_slab, 1.0, 0.0)).reshape(margin_rows, 1, 1)
            target = target * active
            factors_x = line_factors(local, active, 1)
            factors_y = line_factors(local, active, 2)
            factors_z = line_factors(local, active, 0)
            estimate = jnp.zeros_like(target)
            for round_index in range(ROUNDS):
                weight_now = relax_weight(round_index)
                for factors, line_axis in ((factors_x, 1), (factors_y, 2), (factors_z, 0)):
                    update = active * (target - operate(local, estimate))
                    estimate = correction_step(factors, line_axis, update, weight_now, estimate)
            piece = lax.dynamic_slice_in_dim(combined, start, margin_rows, 0) + weight * estimate
            return lax.dynamic_update_slice_in_dim(combined, piece, start, 0)

        combined = lax.fori_loop(0, N_SUB, one_slab, jnp.zeros((NZ + 2 * OV, NX, NY), jnp.float32))
        pressure = pressure + combined[OV:OV + NZ]
    return pressure
```

```python
import functools
import math

import jax
import jax.numpy as jnp
from jax import lax
from jax.experimental import pallas as pl
from jax.experimental.pallas import tpu as pltpu
from jax.sharding import PartitionSpec as P

OV = 4
BL = 8
ROUNDS = 4
OUTER = 2
FACIES = 8
STORE = 0.02
MESH = pl.DeviceIdType.MESH

OWN = 16
ROWS = OWN + 2 * OV
WIDE = ROWS + 2
LANES = 128
CHUNKS = ROWS // BL
CH = BL * 8

DIRS = ((-1, 0), (1, 0), (0, -1), (0, 1), (-1, -1), (-1, 1), (1, -1), (1, 1))
OPP = tuple(DIRS.index((-a, -b)) for a, b in DIRS)


def relax_weight(k):
    return 1.0 / (1.4 + 0.6 * math.cos(math.pi * (2 * k + 1) / (2 * ROUNDS)))


def harmonic(a, b):
    return 2.0 * a * b / jnp.maximum(a + b, 1e-30)


def roll_x(v, s):
    return pltpu.roll(v.reshape(v.shape[0] // 8, 8, LANES), s % 8, 1).reshape(v.shape)


def roll_y(v, s):
    return pltpu.roll(v, s % LANES, 1)


def roll_z(v, s):
    return pltpu.roll(v, s % v.shape[0], 0)


def reduce_factors(low, high, roll):
    l, u, d = -low, -high, None
    parts = []
    for s in (1, 2, 4):
        if d is None:
            a, b, d = low, high, jnp.ones_like(low)
        else:
            rd = 1.0 / d
            a, b = -l * roll(rd, s), -u * roll(rd, -s)
        d = d + a * roll(u, s) + b * roll(l, -s)
        l, u = a * roll(l, s), b * roll(u, -s)
        parts += [a, b]
    return parts + [1.0 / d]


def reduce_x(r, f):
    a1, b1, a2, b2, c3, iv = f
    r = r + a1 * roll_x(r, 1) + b1 * roll_x(r, -1)
    r = r + a2 * roll_x(r, 2) + b2 * roll_x(r, -2)
    r = r + c3 * roll_x(r, 4)
    return r * iv


def reduce_y(r, f):
    a1, b1, a2, b2, a3, b3, iv = f
    r = r + a1 * roll_y(r, 1) + b1 * roll_y(r, -1)
    r = r + a2 * roll_y(r, 2) + b2 * roll_y(r, -2)
    r = r + a3 * roll_y(r, 4) + b3 * roll_y(r, -4)
    return r * iv


def col(x, planes=ROWS, first=0):
    return pl.ds(first * 8 + x, planes, stride=8)


def kernel(
    fac, fperm, pscale, src, p0, depth, out,
    zs, xs, ds, zr, xr, dr, mx, mzr, mxr, mdr, fzr, cs, cr,
    perm, pres, sper, spre, isrc, tgt, tside, e0, e1, e2, ub, corr,
    co, xf, yf, zf, gx, cx, sco, syf,
    i_send, i_recv, m_send, m_recv, f_send, f_recv, c_send, c_recv,
):
    n_sub, n_grp = lax.axis_size("sub"), lax.axis_size("grp")
    sub, grp = lax.axis_index("sub"), lax.axis_index("grp")
    has_axis = {
        (-1, 0): sub > 0,
        (1, 0): sub < n_sub - 1,
        (0, -1): grp > 0,
        (0, 1): grp < n_grp - 1,
    }
    has = []
    for dz, dx in DIRS:
        if dz and dx:
            has.append(jnp.logical_and(has_axis[(dz, 0)], has_axis[(0, dx)]))
        else:
            has.append(has_axis[(dz, dx)])

    def peer(d):
        return {"sub": sub + DIRS[d][0], "grp": grp + DIRS[d][1]}

    def remote(d, a, b, s_sem, r_sem):
        return pltpu.make_async_remote_copy(
            src_ref=a, dst_ref=b, send_sem=s_sem, recv_sem=r_sem,
            device_id=peer(d), device_id_type=MESH,
        )

    def exchange_start(dirs, make):
        for d in dirs:
            @pl.when(has[d])
            def _(d=d):
                make(d, OPP[d]).start()

    def exchange_wait(dirs, make):
        for d in dirs:
            @pl.when(has[d])
            def _(d=d):
                make(d, OPP[d]).wait_send()
                make(d, d).wait_recv()

    for d in range(8):
        @pl.when(jnp.logical_not(has[d]))
        def _(d=d):
            if d < 2:
                zr[d] = jnp.zeros(zr.shape[1:], jnp.float32)
                mzr[d] = jnp.zeros(mzr.shape[1:], jnp.float32)
                fzr[d] = jnp.zeros(fzr.shape[1:], jnp.float32)
            elif d < 4:
                xr[d - 2] = jnp.zeros(xr.shape[1:], jnp.float32)
                mxr[d - 2] = jnp.zeros(mxr.shape[1:], jnp.float32)
                for ph in range(cr.shape[0]):
                    cr[ph, d - 2] = jnp.zeros(cr.shape[2:], jnp.float32)
            else:
                dr[d - 4] = jnp.zeros(dr.shape[1:], jnp.float32)
                mdr[d - 4] = jnp.zeros(mdr.shape[1:], jnp.float32)

    barrier = pltpu.get_barrier_semaphore()
    for d in range(8):
        @pl.when(has[d])
        def _(d=d):
            pl.semaphore_signal(barrier, inc=1, device_id=peer(d), device_id_type=MESH)

    kinds = fac[...]
    own = jnp.zeros(kinds.shape, jnp.float32)
    for kind in range(FACIES):
        own = jnp.where(kinds == kind, fperm[kind], own)
    own = (own * pscale[...]).reshape(OWN * 8, LANES)
    perm[pl.ds(40, OWN * 8)] = own
    pres[pl.ds(40, OWN * 8)] = p0[...].reshape(OWN * 8, LANES)
    isrc[pl.ds(32, OWN * 8)] = src[...].reshape(OWN * 8, LANES)
    for s in range(2):
        at = 5 if s == 0 else 16
        zs[s, pl.ds(0, 40)] = perm[pl.ds(at * 8, 40)]
        zs[s, pl.ds(40, 40)] = pres[pl.ds(at * 8, 40)]
        zs[s, pl.ds(80, 32)] = isrc[pl.ds(32 if s == 0 else 128, 32)]
        near, far = (0, 1) if s == 0 else (7, 6)
        kn, kf, pn = perm[col(near, 16, 5)], perm[col(far, 16, 5)], pres[col(near, 16, 5)]
        xs[s, pl.ds(0, 16)] = kn
        xs[s, pl.ds(16, 16)] = kf
        xs[s, pl.ds(32, 16)] = pn
        for z in range(2):
            at_rows = 5 if z == 0 else 13
            ds[2 * z + s, pl.ds(0, 8)] = perm[col(near, 8, at_rows)]
            ds[2 * z + s, pl.ds(8, 8)] = perm[col(far, 8, at_rows)]
            ds[2 * z + s, pl.ds(16, 8)] = pres[col(near, 8, at_rows)]

    def init_copy(d, slot):
        if d < 2:
            a, b = zs.at[d], zr.at[slot]
        elif d < 4:
            a, b = xs.at[d - 2], xr.at[slot - 2]
        else:
            a, b = ds.at[d - 4], dr.at[slot - 4]
        return remote(d, a, b, i_send.at[d], i_recv.at[slot])

    pl.semaphore_wait(barrier, sum(jnp.where(h, 1, 0) for h in has))
    exchange_start(range(8), init_copy)

    low = jnp.where(sub > 0, depth[jnp.maximum(sub - 1, 0)], 0)
    high = jnp.where(sub < n_sub - 1, depth[jnp.minimum(sub, n_sub - 2)], 0)

    def active(rows):
        inside = (rows >= OV - low) & (rows < OV + OWN + high)
        return jnp.where(inside, 1.0, 0.0)

    def rows_of(c):
        return lax.broadcasted_iota(jnp.int32, (8, 8, LANES), 0).reshape(CH, LANES) + 8 * c

    lane = lax.broadcasted_iota(jnp.int32, (CH, LANES), 1)
    lane2 = lax.broadcasted_iota(jnp.int32, (ROWS, LANES), 1)
    row2 = lax.broadcasted_iota(jnp.int32, (ROWS, LANES), 0)
    subl = lax.broadcasted_iota(jnp.int32, (8, 8, LANES), 1).reshape(CH, LANES)
    zeros_plane = jnp.zeros((8, LANES), jnp.float32)
    for e in (e0, e1, e2):
        e[pl.ds(0, 8)] = zeros_plane
        e[pl.ds((ROWS + 1) * 8, 8)] = zeros_plane

    exchange_wait(range(8), init_copy)

    perm[pl.ds(0, 40)] = zr[0, pl.ds(0, 40)]
    pres[pl.ds(0, 40)] = zr[0, pl.ds(40, 40)]
    isrc[pl.ds(0, 32)] = zr[0, pl.ds(80, 32)]
    perm[pl.ds(168, 40)] = zr[1, pl.ds(0, 40)]
    pres[pl.ds(168, 40)] = zr[1, pl.ds(40, 40)]
    isrc[pl.ds(160, 32)] = zr[1, pl.ds(80, 32)]
    for s in range(2):
        for f in range(2):
            sper[s, f, pl.ds(5, 16)] = xr[s, pl.ds(16 * f, 16)]
            sper[s, f, pl.ds(0, 5)] = dr[s, pl.ds(8 * f + 3, 5)]
            sper[s, f, pl.ds(21, 5)] = dr[2 + s, pl.ds(8 * f, 5)]
        spre[s, pl.ds(4, 16)] = xr[s, pl.ds(32, 16)]
        spre[s, pl.ds(0, 4)] = dr[s, pl.ds(20, 4)]
        spre[s, pl.ds(20, 4)] = dr[2 + s, pl.ds(16, 4)]
        ub[col(7 * s)] = sper[s, 0, pl.ds(1, ROWS)]

    for c in range(CHUNKS):
        here = pl.ds(c * CH, CH)
        mid = perm[pl.ds((c * 8 + 1) * 8, CH)]
        edge = ub[here]
        fb = harmonic(perm[pl.ds(c * CH, CH)], mid)
        fa = harmonic(mid, perm[pl.ds((c * 8 + 2) * 8, CH)])
        fl = harmonic(jnp.where(subl == 0, edge, roll_x(mid, 1)), mid)
        fr = harmonic(mid, jnp.where(subl == 7, edge, roll_x(mid, -1)))
        ff = harmonic(jnp.where(lane == 0, 0.0, roll_y(mid, 1)), mid)
        fk = harmonic(mid, jnp.where(lane == LANES - 1, 0.0, roll_y(mid, -1)))
        act = active(rows_of(c))
        inv = act / (STORE + fb + fa + fl + fr + ff + fk)
        fl, fr = fl * inv, fr * inv
        ub[here] = jnp.where(subl == 0, fl, fr)
        fl, fr = jnp.where(subl == 0, 0.0, fl), jnp.where(subl == 7, 0.0, fr)
        fb, fa, ff, fk = fb * inv, fa * inv, ff * inv, fk * inv
        for i, f in enumerate((fb, fa, fl, fr, ff, fk)):
            co[i, here] = f
        isrc[here] = isrc[here] * inv
        a1, b1, a2, b2, a3, b3, iv = reduce_factors(fl, fr, roll_x)
        for i, f in enumerate((a2, b2, a3 + b3, iv)):
            xf[i, here] = f
        fy = reduce_factors(
            jnp.where(lane % BL == 0, 0.0, ff), jnp.where(lane % BL == BL - 1, 0.0, fk), roll_y
        )
        for i, f in enumerate(fy):
            yf[i, here] = f
        lz = -fb * active(rows_of(c) - 1)
        uz = -fa * active(rows_of(c) + 1)
        d = None
        for i in range(BL):
            at = pl.ds(c * CH + i * 8, 8)
            part = slice(i * 8, i * 8 + 8)
            if i == 0:
                m, d = zeros_plane, jnp.ones((8, LANES), jnp.float32)
            else:
                m = lz[part] / d
                d = 1.0 - m * uz[(i - 1) * 8 : i * 8]
            zf[0, at] = m
            zf[1, at] = 1.0 / d
            zf[2, at] = uz[part] / d
    for s in range(2):
        cx[s] = ub[col(7 * s)]

    def xfac(here):
        return [co[2, here], co[3, here]] + [xf[i, here] for i in range(4)]

    for c in range(CHUNKS):
        here = pl.ds(c * CH, CH)
        edge, f = ub[here], xfac(here)
        for s in range(2):
            gx[s, here] = reduce_x(jnp.where(subl == 7 * s, edge, 0.0), f)

    for s in range(2):
        mid = sper[s, 0, pl.ds(1, ROWS)]
        fb = harmonic(sper[s, 0, pl.ds(0, ROWS)], mid)
        fa = harmonic(mid, sper[s, 0, pl.ds(2, ROWS)])
        fx = harmonic(mid, sper[s, 1, pl.ds(1, ROWS)])
        fo = harmonic(mid, perm[col(7 * s, ROWS, 1)])
        ff = harmonic(jnp.where(lane2 == 0, 0.0, roll_y(mid, 1)), mid)
        fk = harmonic(mid, jnp.where(lane2 == LANES - 1, 0.0, roll_y(mid, -1)))
        inv = active(row2) / (STORE + fb + fa + fx + fo + ff + fk)
        fb = jnp.where(row2 == 0, 0.0, fb * inv)
        fa = jnp.where(row2 == ROWS - 1, 0.0, fa * inv)
        ff, fk = ff * inv, fk * inv
        for i, f in enumerate((fb, fa, fx * inv, fo * inv, ff, fk)):
            sco[s, i] = f
        fy = reduce_factors(
            jnp.where(lane2 % BL == 0, 0.0, ff), jnp.where(lane2 % BL == BL - 1, 0.0, fk), roll_y
        )
        for i, f in enumerate(fy):
            syf[s, i] = f

    def update(t, e, c, scale=None):
        here = pl.ds(c * CH, CH)
        v = e[pl.ds((c * 8 + 1) * 8, CH)]
        u = t[here] - (v if scale is None else v * scale)
        u = u + co[0, here] * e[pl.ds(c * CH, CH)] + co[1, here] * e[pl.ds((c * 8 + 2) * 8, CH)]
        u = u + co[2, here] * roll_x(v, 1) + co[3, here] * roll_x(v, -1)
        return v, u + co[4, here] * roll_y(v, 1) + co[5, here] * roll_y(v, -1)

    def col_copy(ph, rows):
        def make(d, slot):
            return remote(
                d, cs.at[ph, d - 2, pl.ds(0, rows)], cr.at[ph, slot - 2, pl.ds(0, rows)],
                c_send.at[ph, d - 2], c_recv.at[ph, slot - 2],
            )
        return make

    def one_round(outer, k):
        first = isinstance(k, int)
        ph = outer * 2 * ROUNDS + 2 * k
        om = relax_weight(0)
        if not first:
            for i in range(1, ROUNDS):
                om = jnp.where(k == i, jnp.float32(relax_weight(i)), om)
        for c in range(CHUNKS):
            here = pl.ds(c * CH, CH)
            if first:
                e1[pl.ds((c * 8 + 1) * 8, CH)] = om * reduce_x(tgt[here], xfac(here))
            else:
                v, u = update(tgt, e0, c)
                e1[pl.ds((c * 8 + 1) * 8, CH)] = v + om * reduce_x(u, xfac(here))
        if not first:
            exchange_wait((2, 3), col_copy(ph, ROWS))
            for z in range(ROWS):
                at, here = pl.ds((z + 1) * 8, 8), pl.ds(z * 8, 8)
                left = jnp.broadcast_to(cr[ph, 0, pl.ds(z, 1)], (8, LANES))
                right = jnp.broadcast_to(cr[ph, 1, pl.ds(z, 1)], (8, LANES))
                e1[at] = e1[at] + om * (gx[0, here] * left + gx[1, here] * right)
        ph = ph + 1
        for s in range(2):
            near, far = (0, 1) if s == 0 else (7, 6)
            cs[ph, s, pl.ds(0, ROWS)] = e1[col(near, ROWS, 1)]
            cs[ph, s, pl.ds(ROWS, ROWS)] = e1[col(far, ROWS, 1)]
            if first:
                cs[ph, s, pl.ds(2 * ROWS, ROWS)] = tgt[col(near)]
        make = col_copy(ph, (3 if first else 2) * ROWS)
        exchange_start((2, 3), make)
        for c in range(CHUNKS):
            here = pl.ds(c * CH, CH)
            v, u = update(tgt, e1, c)
            e2[pl.ds((c * 8 + 1) * 8, CH)] = v + om * reduce_y(u, [yf[i, here] for i in range(7)])
        exchange_wait((2, 3), make)
        beside = []
        for s in range(2):
            near, far = cr[ph, s, pl.ds(0, ROWS)], cr[ph, s, pl.ds(ROWS, ROWS)]
            if first:
                tside[s] = cr[ph, s, pl.ds(2 * ROWS, ROWS)]
            inner = e1[col(7 * s, ROWS, 1)]
            u = tside[s] - near
            u = u + sco[s, 0] * roll_z(near, 1) + sco[s, 1] * roll_z(near, -1)
            u = u + sco[s, 2] * far + sco[s, 3] * inner
            u = u + sco[s, 4] * roll_y(near, 1) + sco[s, 5] * roll_y(near, -1)
            beside.append(near + om * reduce_y(u, [syf[s, i] for i in range(7)]))
            f = [yf[i, col(7 * s)] for i in range(7)]
            at = col(7 * s, ROWS, 1)
            e2[at] = e2[at] + om * reduce_y(cx[s] * near, f)
        for c in range(CHUNKS):
            ub[pl.ds(c * CH, CH)] = update(tgt, e2, c)[1]
        for s in range(2):
            at = col(7 * s)
            ub[at] = ub[at] + cx[s] * beside[s]
        for c in range(CHUNKS):
            fw, prev = [], None
            for i in range(BL):
                at = pl.ds(c * CH + i * 8, 8)
                prev = ub[at] if i == 0 else ub[at] - zf[0, at] * prev
                fw.append(prev)
            nxt = None
            for i in range(BL - 1, -1, -1):
                at = pl.ds(c * CH + i * 8, 8)
                nxt = fw[i] * zf[1, at] if nxt is None else fw[i] * zf[1, at] - zf[2, at] * nxt
                to = pl.ds((c * 8 + i + 1) * 8, 8)
                e0[to] = e2[to] + om * nxt

        def send_next():
            for s in range(2):
                cs[ph + 1, s, pl.ds(0, ROWS)] = e0[col(7 * s, ROWS, 1)]
            exchange_start((2, 3), col_copy(ph + 1, ROWS))

        if first:
            send_next()
        else:
            pl.when(k < ROUNDS - 1)(send_next)

    def mid_copy(d, slot):
        if d < 2:
            a, b = corr.at[pl.ds(0 if d == 0 else 120, 72)], mzr.at[slot]
        elif d < 4:
            a, b = mx.at[d - 2], mxr.at[slot - 2]
        else:
            z, s = divmod(d - 4, 2)
            a, b = mx.at[s, pl.ds(16 * z, 8)], mdr.at[slot - 4]
        return remote(d, a, b, m_send.at[d], m_recv.at[slot])

    def end_copy(d, slot):
        a = corr.at[pl.ds(0 if d == 0 else 160, 32)]
        return remote(d, a, fzr.at[slot], f_send.at[d], f_recv.at[slot])

    for outer in range(OUTER):
        for c in range(CHUNKS):
            tgt[pl.ds(c * CH, CH)] = update(isrc, pres, c, active(rows_of(c)))[1]
        for s in range(2):
            tgt[col(7 * s)] = tgt[col(7 * s)] + cx[s] * spre[s]
        one_round(outer, 0)

        def step(k, carry, outer=outer):
            one_round(outer, k)
            return carry

        lax.fori_loop(1, ROUNDS, step, 0)
        for c in range(CHUNKS):
            rows = rows_of(c)
            band = (rows < OV + low) | (rows >= OV + OWN - high)
            w = active(rows) * jnp.where(band, 0.5, 1.0)
            corr[pl.ds(c * CH, CH)] = w * e0[pl.ds((c * 8 + 1) * 8, CH)]
        if outer == 0:
            for s in range(2):
                mx[s] = corr[col(7 * s)]
            exchange_start(range(8), mid_copy)
            pres[pl.ds(8, ROWS * 8)] = pres[pl.ds(8, ROWS * 8)] + corr[...]
            exchange_wait(range(8), mid_copy)
            for z in range(2):
                at = pl.ds(0 if z == 0 else 17 * 8, 72)
                pres[at] = pres[at] + mzr[z]
            for s in range(2):
                spre[s] = spre[s] + mxr[s]
                for z in range(2):
                    at = pl.ds(16 * z, 8)
                    spre[s, at] = spre[s, at] + mdr[2 * z + s]
        else:
            exchange_start((0, 1), end_copy)
            pres[pl.ds(8, ROWS * 8)] = pres[pl.ds(8, ROWS * 8)] + corr[...]
            exchange_wait((0, 1), end_copy)
            for z in range(2):
                at = pl.ds(40 if z == 0 else 17 * 8, 32)
                pres[at] = pres[at] + fzr[z]
    out[...] = pres[pl.ds(40, OWN * 8)].reshape(OWN, 8, LANES)


def on_device(facies, facies_perm, perm_scale, source, pressure_start, intersection_depth):
    assert source.shape == (OWN, 8, LANES)
    f32 = jnp.float32

    def buf(*shape):
        return pltpu.VMEM(shape, f32)

    field, wide = (ROWS * 8, LANES), (WIDE * 8, LANES)
    phases = OUTER * 2 * ROUNDS
    scratch = [
        buf(2, 112, LANES), buf(2, 48, LANES), buf(4, 24, LANES),
        buf(2, 112, LANES), buf(2, 48, LANES), buf(4, 24, LANES),
        buf(2, ROWS, LANES), buf(2, 72, LANES), buf(2, ROWS, LANES), buf(4, 8, LANES),
        buf(2, 32, LANES), buf(phases, 2, 3 * ROWS, LANES), buf(phases, 2, 3 * ROWS, LANES),
        buf(*wide), buf(*wide), buf(2, 2, 32, LANES), buf(2, ROWS, LANES),
        buf(*field), buf(*field), buf(2, ROWS, LANES),
        buf(*wide), buf(*wide), buf(*wide), buf(*field), buf(*field),
        buf(6, *field), buf(4, *field), buf(7, *field), buf(3, *field),
        buf(2, *field), buf(2, ROWS, LANES), buf(2, 6, ROWS, LANES), buf(2, 7, ROWS, LANES),
    ]
    sems = [pltpu.SemaphoreType.DMA((n,)) for n in (8, 8, 8, 8, 2, 2)]
    sems += [pltpu.SemaphoreType.DMA((phases, 2)) for _ in range(2)]
    vmem, smem = pl.BlockSpec(memory_space=pltpu.VMEM), pl.BlockSpec(memory_space=pltpu.SMEM)
    return pl.pallas_call(
        kernel,
        out_shape=jax.ShapeDtypeStruct(source.shape, f32),
        in_specs=[vmem, smem, vmem, vmem, vmem, smem],
        out_specs=vmem,
        scratch_shapes=scratch + sems,
        compiler_params=pltpu.CompilerParams(
            collective_id=0, has_side_effects=True, vmem_limit_bytes=32 * 1024 * 1024
        ),
        name="schwarz",
    )(facies, facies_perm, perm_scale, source, pressure_start, intersection_depth)


def solution(mesh):
    return jax.shard_map(
        on_device,
        mesh=mesh,
        in_specs=(
            P("sub", "grp", None),
            P(),
            P("sub", "grp", None),
            P("sub", "grp", None),
            P("sub", "grp", None),
            P(),
        ),
        out_specs=P("sub", "grp", None),
        check_vma=False,
    )
```

```python
import functools
import math

import jax
import jax.numpy as jnp
from jax import lax
from jax.experimental import pallas as pl
from jax.experimental.pallas import tpu as pltpu
from jax.sharding import PartitionSpec as P

OV = 4
BL = 8
ROUNDS = 4
OUTER = 2
FACIES = 8
STORE = 0.02
MESH = pl.DeviceIdType.MESH

OWN = 16
ROWS = OWN + 2 * OV
WIDE = ROWS + 2
LANES = 128
CHUNKS = ROWS // BL
CH = BL * 8

DIRS = (
    (-1, 0), (1, 0), (0, -1), (0, 1), (-1, -1), (-1, 1), (1, -1), (1, 1), (0, -2), (0, 2)
)
OPP = tuple(DIRS.index((-a, -b)) for a, b in DIRS)


def relax_weight(k):
    return 1.0 / (1.4 + 0.6 * math.cos(math.pi * (2 * k + 1) / (2 * ROUNDS)))


def harmonic(a, b):
    return 2.0 * a * b / jnp.maximum(a + b, 1e-30)


def roll_x(v, s):
    return pltpu.roll(v.reshape(v.shape[0] // 8, 8, LANES), s % 8, 1).reshape(v.shape)


def roll_y(v, s):
    return pltpu.roll(v, s % LANES, 1)


def roll_z(v, s):
    return pltpu.roll(v, s % v.shape[0], 0)


def reduce_factors(low, high, roll):
    l, u, d = -low, -high, None
    parts = []
    for s in (1, 2, 4):
        if d is None:
            a, b, d = low, high, jnp.ones_like(low)
        else:
            rd = 1.0 / d
            a, b = -l * roll(rd, s), -u * roll(rd, -s)
        d = d + a * roll(u, s) + b * roll(l, -s)
        l, u = a * roll(l, s), b * roll(u, -s)
        parts += [a, b]
    return parts + [1.0 / d]


def reduce_x(r, f):
    a1, b1, a2, b2, c3, iv = f
    r = r + a1 * roll_x(r, 1) + b1 * roll_x(r, -1)
    r = r + a2 * roll_x(r, 2) + b2 * roll_x(r, -2)
    r = r + c3 * roll_x(r, 4)
    return r * iv


def reduce_y(r, f):
    a1, b1, a2, b2, a3, b3, iv = f
    r = r + a1 * roll_y(r, 1) + b1 * roll_y(r, -1)
    r = r + a2 * roll_y(r, 2) + b2 * roll_y(r, -2)
    r = r + a3 * roll_y(r, 4) + b3 * roll_y(r, -4)
    return r * iv


def col(x, planes=ROWS, first=0):
    return pl.ds(first * 8 + x, planes, stride=8)


def kernel(
    fac_h, fperm_h, pscale_h, src_h, p0_h, depth_h, out,
    fac, pscale, src, p0, fperm, depth, in_sem, gs, gr, c2r,
    zs, xs, ds, zr, xr, dr, mx, mzr, mxr, mdr, fzr, cs, cr,
    perm, pres, sper, spre, isrc, tgt, tside, e0, e1, e2, ub, corr,
    co, xf, yf, zf, gx, cx, sco, syf,
    i_send, i_recv, m_send, m_recv, f_send, f_recv, g_send, g_recv,
    c_send, c_recv, c2_send, c2_recv,
):
    n_sub, n_grp = lax.axis_size("sub"), lax.axis_size("grp")
    sub, grp = lax.axis_index("sub"), lax.axis_index("grp")
    has_axis = {
        (-1, 0): sub > 0,
        (1, 0): sub < n_sub - 1,
        (0, -1): grp > 0,
        (0, 1): grp < n_grp - 1,
        (0, -2): grp > 1,
        (0, 2): grp < n_grp - 2,
    }
    has = []
    for dz, dx in DIRS:
        if dz and dx:
            has.append(jnp.logical_and(has_axis[(dz, 0)], has_axis[(0, dx)]))
        else:
            has.append(has_axis[(dz, dx)])

    def peer(d):
        return {"sub": sub + DIRS[d][0], "grp": grp + DIRS[d][1]}

    def remote(d, a, b, s_sem, r_sem):
        return pltpu.make_async_remote_copy(
            src_ref=a, dst_ref=b, send_sem=s_sem, recv_sem=r_sem,
            device_id=peer(d), device_id_type=MESH,
        )

    def exchange_start(dirs, make):
        for d in dirs:
            @pl.when(has[d])
            def _(d=d):
                make(d, OPP[d]).start()

    def exchange_wait(dirs, make):
        for d in dirs:
            @pl.when(has[d])
            def _(d=d):
                make(d, OPP[d]).wait_send()
                make(d, d).wait_recv()

    barrier = pltpu.get_barrier_semaphore()
    for d in range(len(DIRS)):
        @pl.when(has[d])
        def _(d=d):
            pl.semaphore_signal(barrier, inc=1, device_id=peer(d), device_id_type=MESH)

    loads = [
        pltpu.make_async_copy(a, b, in_sem.at[i])
        for i, (a, b) in enumerate((
            (fac_h, fac), (pscale_h, pscale), (p0_h, p0), (src_h, src),
            (fperm_h, fperm), (depth_h, depth),
        ))
    ]
    for load in loads:
        load.start()

    for d in range(len(DIRS)):
        @pl.when(jnp.logical_not(has[d]))
        def _(d=d):
            if d < 2:
                zr[d] = jnp.zeros(zr.shape[1:], jnp.float32)
                mzr[d] = jnp.zeros(mzr.shape[1:], jnp.float32)
                fzr[d] = jnp.zeros(fzr.shape[1:], jnp.float32)
            elif d < 4:
                xr[d - 2] = jnp.zeros(xr.shape[1:], jnp.float32)
                mxr[d - 2] = jnp.zeros(mxr.shape[1:], jnp.float32)
                gr[d - 2] = jnp.zeros(gr.shape[1:], jnp.float32)
                for ph in range(cr.shape[0]):
                    cr[ph, d - 2] = jnp.zeros(cr.shape[2:], jnp.float32)
            elif d < 8:
                dr[d - 4] = jnp.zeros(dr.shape[1:], jnp.float32)
                mdr[d - 4] = jnp.zeros(mdr.shape[1:], jnp.float32)
            else:
                for ph in range(c2r.shape[0]):
                    c2r[ph, d - 8] = jnp.zeros(c2r.shape[2:], jnp.float32)

    for load in loads:
        load.wait()

    kinds = fac[...]
    own = jnp.zeros(kinds.shape, jnp.float32)
    for kind in range(FACIES):
        own = jnp.where(kinds == kind, fperm[kind], own)
    own = (own * pscale[...]).reshape(OWN * 8, LANES)
    perm[pl.ds(40, OWN * 8)] = own
    pres[pl.ds(40, OWN * 8)] = p0[...].reshape(OWN * 8, LANES)
    isrc[pl.ds(32, OWN * 8)] = src[...].reshape(OWN * 8, LANES)
    for s in range(2):
        at = 5 if s == 0 else 16
        zs[s, pl.ds(0, 40)] = perm[pl.ds(at * 8, 40)]
        zs[s, pl.ds(40, 40)] = pres[pl.ds(at * 8, 40)]
        zs[s, pl.ds(80, 32)] = isrc[pl.ds(32 if s == 0 else 128, 32)]
        near, far = (0, 1) if s == 0 else (7, 6)
        kn, kf, pn = perm[col(near, 16, 5)], perm[col(far, 16, 5)], pres[col(near, 16, 5)]
        xs[s, pl.ds(0, 16)] = kn
        xs[s, pl.ds(16, 16)] = kf
        xs[s, pl.ds(32, 16)] = pn
        for z in range(2):
            at_rows = 5 if z == 0 else 13
            ds[2 * z + s, pl.ds(0, 8)] = perm[col(near, 8, at_rows)]
            ds[2 * z + s, pl.ds(8, 8)] = perm[col(far, 8, at_rows)]
            ds[2 * z + s, pl.ds(16, 8)] = pres[col(near, 8, at_rows)]

    def init_copy(d, slot):
        if d < 2:
            a, b = zs.at[d], zr.at[slot]
        elif d < 4:
            a, b = xs.at[d - 2], xr.at[slot - 2]
        else:
            a, b = ds.at[d - 4], dr.at[slot - 4]
        return remote(d, a, b, i_send.at[d], i_recv.at[slot])

    pl.semaphore_wait(barrier, sum(jnp.where(h, 1, 0) for h in has))
    exchange_start(range(8), init_copy)

    low = jnp.where(sub > 0, depth[jnp.maximum(sub - 1, 0)], 0)
    high = jnp.where(sub < n_sub - 1, depth[jnp.minimum(sub, n_sub - 2)], 0)

    def active(rows):
        inside = (rows >= OV - low) & (rows < OV + OWN + high)
        return jnp.where(inside, 1.0, 0.0)

    def rows_of(c):
        return lax.broadcasted_iota(jnp.int32, (8, 8, LANES), 0).reshape(CH, LANES) + 8 * c

    lane = lax.broadcasted_iota(jnp.int32, (CH, LANES), 1)
    lane2 = lax.broadcasted_iota(jnp.int32, (ROWS, LANES), 1)
    row2 = lax.broadcasted_iota(jnp.int32, (ROWS, LANES), 0)
    subl = lax.broadcasted_iota(jnp.int32, (8, 8, LANES), 1).reshape(CH, LANES)
    zeros_plane = jnp.zeros((8, LANES), jnp.float32)
    for e in (e0, e1, e2):
        e[pl.ds(0, 8)] = zeros_plane
        e[pl.ds((ROWS + 1) * 8, 8)] = zeros_plane

    exchange_wait(range(8), init_copy)

    perm[pl.ds(0, 40)] = zr[0, pl.ds(0, 40)]
    pres[pl.ds(0, 40)] = zr[0, pl.ds(40, 40)]
    isrc[pl.ds(0, 32)] = zr[0, pl.ds(80, 32)]
    perm[pl.ds(168, 40)] = zr[1, pl.ds(0, 40)]
    pres[pl.ds(168, 40)] = zr[1, pl.ds(40, 40)]
    isrc[pl.ds(160, 32)] = zr[1, pl.ds(80, 32)]
    for s in range(2):
        for f in range(2):
            sper[s, f, pl.ds(5, 16)] = xr[s, pl.ds(16 * f, 16)]
            sper[s, f, pl.ds(0, 5)] = dr[s, pl.ds(8 * f + 3, 5)]
            sper[s, f, pl.ds(21, 5)] = dr[2 + s, pl.ds(8 * f, 5)]
        spre[s, pl.ds(4, 16)] = xr[s, pl.ds(32, 16)]
        spre[s, pl.ds(0, 4)] = dr[s, pl.ds(20, 4)]
        spre[s, pl.ds(20, 4)] = dr[2 + s, pl.ds(16, 4)]
        ub[col(7 * s)] = sper[s, 0, pl.ds(1, ROWS)]

    for c in range(CHUNKS):
        here = pl.ds(c * CH, CH)
        mid = perm[pl.ds((c * 8 + 1) * 8, CH)]
        edge = ub[here]
        fb = harmonic(perm[pl.ds(c * CH, CH)], mid)
        fa = harmonic(mid, perm[pl.ds((c * 8 + 2) * 8, CH)])
        fl = harmonic(jnp.where(subl == 0, edge, roll_x(mid, 1)), mid)
        fr = harmonic(mid, jnp.where(subl == 7, edge, roll_x(mid, -1)))
        ff = harmonic(jnp.where(lane == 0, 0.0, roll_y(mid, 1)), mid)
        fk = harmonic(mid, jnp.where(lane == LANES - 1, 0.0, roll_y(mid, -1)))
        act = active(rows_of(c))
        inv = act / (STORE + fb + fa + fl + fr + ff + fk)
        fl, fr = fl * inv, fr * inv
        ub[here] = jnp.where(subl == 0, fl, fr)
        fl, fr = jnp.where(subl == 0, 0.0, fl), jnp.where(subl == 7, 0.0, fr)
        fb, fa, ff, fk = fb * inv, fa * inv, ff * inv, fk * inv
        for i, f in enumerate((fb, fa, fl, fr, ff, fk)):
            co[i, here] = f
        isrc[here] = isrc[here] * inv
        a1, b1, a2, b2, a3, b3, iv = reduce_factors(fl, fr, roll_x)
        for i, f in enumerate((a2, b2, a3 + b3, iv)):
            xf[i, here] = f
        fy = reduce_factors(
            jnp.where(lane % BL == 0, 0.0, ff), jnp.where(lane % BL == BL - 1, 0.0, fk), roll_y
        )
        for i, f in enumerate(fy):
            yf[i, here] = f
        lz = -fb * active(rows_of(c) - 1)
        uz = -fa * active(rows_of(c) + 1)
        d = None
        for i in range(BL):
            at = pl.ds(c * CH + i * 8, 8)
            part = slice(i * 8, i * 8 + 8)
            if i == 0:
                m, d = zeros_plane, jnp.ones((8, LANES), jnp.float32)
            else:
                m = lz[part] / d
                d = 1.0 - m * uz[(i - 1) * 8 : i * 8]
            zf[0, at] = m
            zf[1, at] = 1.0 / d
            zf[2, at] = uz[part] / d
    for s in range(2):
        cx[s] = ub[col(7 * s)]

    def xfac(here):
        return [co[2, here], co[3, here]] + [xf[i, here] for i in range(4)]

    for c in range(CHUNKS):
        here = pl.ds(c * CH, CH)
        edge, f = ub[here], xfac(here)
        for s in range(2):
            gx[s, here] = reduce_x(jnp.where(subl == 7 * s, edge, 0.0), f)
        ub[here] = jnp.zeros((CH, LANES), jnp.float32)
    for s in range(2):
        near, far = (0, 1) if s == 0 else (7, 6)
        for i in range(2):
            gs[s, pl.ds(2 * i * ROWS, ROWS)] = gx[i, col(near)]
            gs[s, pl.ds((2 * i + 1) * ROWS, ROWS)] = gx[i, col(far)]

    def answer_copy(d, slot):
        return remote(
            d, gs.at[d - 2], gr.at[slot - 2], g_send.at[d - 2], g_recv.at[slot - 2]
        )

    exchange_start((2, 3), answer_copy)

    for s in range(2):
        mid = sper[s, 0, pl.ds(1, ROWS)]
        fb = harmonic(sper[s, 0, pl.ds(0, ROWS)], mid)
        fa = harmonic(mid, sper[s, 0, pl.ds(2, ROWS)])
        fx = harmonic(mid, sper[s, 1, pl.ds(1, ROWS)])
        fo = harmonic(mid, perm[col(7 * s, ROWS, 1)])
        ff = harmonic(jnp.where(lane2 == 0, 0.0, roll_y(mid, 1)), mid)
        fk = harmonic(mid, jnp.where(lane2 == LANES - 1, 0.0, roll_y(mid, -1)))
        inv = active(row2) / (STORE + fb + fa + fx + fo + ff + fk)
        fb = jnp.where(row2 == 0, 0.0, fb * inv)
        fa = jnp.where(row2 == ROWS - 1, 0.0, fa * inv)
        ff, fk = ff * inv, fk * inv
        for i, f in enumerate((fb, fa, fx * inv, fo * inv, ff, fk)):
            sco[s, i] = f
        fy = reduce_factors(
            jnp.where(lane2 % BL == 0, 0.0, ff), jnp.where(lane2 % BL == BL - 1, 0.0, fk), roll_y
        )
        for i, f in enumerate(fy):
            syf[s, i] = f

    def update(t, e, c, scale=None):
        here = pl.ds(c * CH, CH)
        v = e[pl.ds((c * 8 + 1) * 8, CH)]
        u = t[here] - (v if scale is None else v * scale)
        u = u + co[0, here] * e[pl.ds(c * CH, CH)] + co[1, here] * e[pl.ds((c * 8 + 2) * 8, CH)]
        u = u + co[2, here] * roll_x(v, 1) + co[3, here] * roll_x(v, -1)
        return v, u + co[4, here] * roll_y(v, 1) + co[5, here] * roll_y(v, -1)

    def col_copy(ph):
        def make(d, slot):
            if d < 4:
                return remote(
                    d, cs.at[ph, d - 2], cr.at[ph, slot - 2],
                    c_send.at[ph, d - 2], c_recv.at[ph, slot - 2],
                )
            return remote(
                d, cs.at[ph, d - 8, pl.ds(2 * ROWS, ROWS)], c2r.at[ph, slot - 8],
                c2_send.at[ph, d - 8], c2_recv.at[ph, slot - 8],
            )
        return make

    def one_round(outer, k):
        first = isinstance(k, int)
        ph = outer * ROUNDS + k
        om = relax_weight(0)
        if not first:
            for i in range(1, ROUNDS):
                om = jnp.where(k == i, jnp.float32(relax_weight(i)), om)
        for c in range(CHUNKS):
            here = pl.ds(c * CH, CH)
            if first:
                e1[pl.ds((c * 8 + 1) * 8, CH)] = om * reduce_x(tgt[here], xfac(here))
            else:
                v, u = update(tgt, e0, c)
                e1[pl.ds((c * 8 + 1) * 8, CH)] = v + om * reduce_x(u, xfac(here))
        for s in range(2):
            near, far = (0, 1) if s == 0 else (7, 6)
            cs[ph, s, pl.ds(0, ROWS)] = e1[col(near, ROWS, 1)]
            cs[ph, s, pl.ds(ROWS, ROWS)] = e1[col(far, ROWS, 1)]
            if first:
                cs[ph, s, pl.ds(2 * ROWS, ROWS)] = tgt[col(near)]
            else:
                cs[ph, s, pl.ds(2 * ROWS, ROWS)] = e0[col(near, ROWS, 1)]
        dirs = (2, 3) if first else (2, 3, 8, 9)
        exchange_start(dirs, col_copy(ph))
        exchange_wait(dirs, col_copy(ph))
        nears, fars = [], []
        for s in range(2):
            near, far = cr[ph, s, pl.ds(0, ROWS)], cr[ph, s, pl.ds(ROWS, ROWS)]
            if first:
                tside[s] = cr[ph, s, pl.ds(2 * ROWS, ROWS)]
            else:
                beyond, inner = c2r[ph, s], e0[col(7 * s, ROWS, 1)]
                left, right = (beyond, inner) if s == 0 else (inner, beyond)
                g = [gr[s, pl.ds(i * ROWS, ROWS)] for i in range(4)]
                near = near + om * (g[0] * left + g[2] * right)
                far = far + om * (g[1] * left + g[3] * right)
            nears.append(near)
            fars.append(far)
            ub[col(7 * s)] = cx[s] * near
        if not first:
            for z in range(ROWS):
                at, here = pl.ds((z + 1) * 8, 8), pl.ds(z * 8, 8)
                left = jnp.broadcast_to(cr[ph, 0, pl.ds(2 * ROWS + z, 1)], (8, LANES))
                right = jnp.broadcast_to(cr[ph, 1, pl.ds(2 * ROWS + z, 1)], (8, LANES))
                e1[at] = e1[at] + om * (gx[0, here] * left + gx[1, here] * right)
        for c in range(CHUNKS):
            here = pl.ds(c * CH, CH)
            v, u = update(tgt, e1, c)
            u = u + ub[here]
            e2[pl.ds((c * 8 + 1) * 8, CH)] = v + om * reduce_y(u, [yf[i, here] for i in range(7)])
        for s in range(2):
            near, far = nears[s], fars[s]
            u = tside[s] - near
            u = u + sco[s, 0] * roll_z(near, 1) + sco[s, 1] * roll_z(near, -1)
            u = u + sco[s, 2] * far + sco[s, 3] * e1[col(7 * s, ROWS, 1)]
            u = u + sco[s, 4] * roll_y(near, 1) + sco[s, 5] * roll_y(near, -1)
            beside = near + om * reduce_y(u, [syf[s, i] for i in range(7)])
            ub[col(7 * s)] = cx[s] * beside
        for c in range(CHUNKS):
            v, u = update(tgt, e2, c)
            u = u + ub[pl.ds(c * CH, CH)]
            fw, prev = [], None
            for i in range(BL):
                at, r = pl.ds(c * CH + i * 8, 8), u[i * 8 : i * 8 + 8]
                prev = r if i == 0 else r - zf[0, at] * prev
                fw.append(prev)
            nxt = None
            for i in range(BL - 1, -1, -1):
                at = pl.ds(c * CH + i * 8, 8)
                nxt = fw[i] * zf[1, at] if nxt is None else fw[i] * zf[1, at] - zf[2, at] * nxt
                e0[pl.ds((c * 8 + i + 1) * 8, 8)] = v[i * 8 : i * 8 + 8] + om * nxt

    def mid_copy(d, slot):
        if d < 2:
            a, b = corr.at[pl.ds(0 if d == 0 else 120, 72)], mzr.at[slot]
        elif d < 4:
            a, b = mx.at[d - 2], mxr.at[slot - 2]
        else:
            z, s = divmod(d - 4, 2)
            a, b = mx.at[s, pl.ds(16 * z, 8)], mdr.at[slot - 4]
        return remote(d, a, b, m_send.at[d], m_recv.at[slot])

    def end_copy(d, slot):
        a = corr.at[pl.ds(0 if d == 0 else 160, 32)]
        return remote(d, a, fzr.at[slot], f_send.at[d], f_recv.at[slot])

    for outer in range(OUTER):
        for s in range(2):
            ub[col(7 * s)] = cx[s] * spre[s]
        for c in range(CHUNKS):
            u = update(isrc, pres, c, active(rows_of(c)))[1]
            tgt[pl.ds(c * CH, CH)] = u + ub[pl.ds(c * CH, CH)]
        one_round(outer, 0)
        if outer == 0:
            exchange_wait((2, 3), answer_copy)

        def step(k, carry, outer=outer):
            one_round(outer, k)
            return carry

        lax.fori_loop(1, ROUNDS, step, 0)
        for c in range(CHUNKS):
            rows = rows_of(c)
            band = (rows < OV + low) | (rows >= OV + OWN - high)
            w = active(rows) * jnp.where(band, 0.5, 1.0)
            corr[pl.ds(c * CH, CH)] = w * e0[pl.ds((c * 8 + 1) * 8, CH)]
        if outer == 0:
            for s in range(2):
                mx[s] = corr[col(7 * s)]
            exchange_start(range(8), mid_copy)
            pres[pl.ds(8, ROWS * 8)] = pres[pl.ds(8, ROWS * 8)] + corr[...]
            exchange_wait(range(8), mid_copy)
            for z in range(2):
                at = pl.ds(0 if z == 0 else 17 * 8, 72)
                pres[at] = pres[at] + mzr[z]
            for s in range(2):
                spre[s] = spre[s] + mxr[s]
                for z in range(2):
                    at = pl.ds(16 * z, 8)
                    spre[s, at] = spre[s, at] + mdr[2 * z + s]
        else:
            exchange_start((0, 1), end_copy)
            pres[pl.ds(8, ROWS * 8)] = pres[pl.ds(8, ROWS * 8)] + corr[...]
            exchange_wait((0, 1), end_copy)
            for z in range(2):
                at = pl.ds(40 if z == 0 else 17 * 8, 32)
                pres[at] = pres[at] + fzr[z]
    out[...] = pres[pl.ds(40, OWN * 8)].reshape(OWN, 8, LANES)


def on_device(facies, facies_perm, perm_scale, source, pressure_start, intersection_depth):
    assert source.shape == (OWN, 8, LANES)
    f32 = jnp.float32

    def buf(*shape):
        return pltpu.VMEM(shape, f32)

    field, wide = (ROWS * 8, LANES), (WIDE * 8, LANES)
    phases, own, dma = OUTER * ROUNDS, source.shape, pltpu.SemaphoreType.DMA
    scratch = [
        pltpu.VMEM(own, jnp.int32), buf(*own), buf(*own), buf(*own),
        pltpu.SMEM(facies_perm.shape, f32), pltpu.SMEM(intersection_depth.shape, jnp.int32),
        dma((6,)), buf(2, 4 * ROWS, LANES), buf(2, 4 * ROWS, LANES), buf(phases, 2, ROWS, LANES),
        buf(2, 112, LANES), buf(2, 48, LANES), buf(4, 24, LANES),
        buf(2, 112, LANES), buf(2, 48, LANES), buf(4, 24, LANES),
        buf(2, ROWS, LANES), buf(2, 72, LANES), buf(2, ROWS, LANES), buf(4, 8, LANES),
        buf(2, 32, LANES), buf(phases, 2, 3 * ROWS, LANES), buf(phases, 2, 3 * ROWS, LANES),
        buf(*wide), buf(*wide), buf(2, 2, 32, LANES), buf(2, ROWS, LANES),
        buf(*field), buf(*field), buf(2, ROWS, LANES),
        buf(*wide), buf(*wide), buf(*wide), buf(*field), buf(*field),
        buf(6, *field), buf(4, *field), buf(7, *field), buf(3, *field),
        buf(2, *field), buf(2, ROWS, LANES), buf(2, 6, ROWS, LANES), buf(2, 7, ROWS, LANES),
    ]
    sems = [dma((n,)) for n in (8, 8, 8, 8, 2, 2, 2, 2)]
    sems += [dma((phases, 2)) for _ in range(4)]
    return pl.pallas_call(
        kernel,
        out_shape=jax.ShapeDtypeStruct(source.shape, f32),
        in_specs=[pl.BlockSpec(memory_space=pl.ANY)] * 6,
        out_specs=pl.BlockSpec(memory_space=pltpu.VMEM),
        scratch_shapes=scratch + sems,
        compiler_params=pltpu.CompilerParams(
            collective_id=0, has_side_effects=True, vmem_limit_bytes=60 * 1024 * 1024
        ),
        name="schwarz",
    )(facies, facies_perm, perm_scale, source, pressure_start, intersection_depth)


def solution(mesh):
    return jax.shard_map(
        on_device,
        mesh=mesh,
        in_specs=(
            P("sub", "grp", None),
            P(),
            P("sub", "grp", None),
            P("sub", "grp", None),
            P("sub", "grp", None),
            P(),
        ),
        out_specs=P("sub", "grp", None),
        check_vma=False,
    )
```

```python
import functools
import math

import jax
import jax.numpy as jnp
from jax import lax
from jax.experimental import pallas as pl
from jax.experimental.pallas import tpu as pltpu
from jax.sharding import PartitionSpec as P

OV = 4
BL = 8
ROUNDS = 4
OUTER = 2
FACIES = 8
STORE = 0.02
MESH = pl.DeviceIdType.MESH

OWN = 16
ROWS = OWN + 2 * OV
WIDE = ROWS + 2
LANES = 128
CHUNKS = ROWS // BL
CH = BL * 8

DIRS = (
    (-1, 0), (1, 0), (0, -1), (0, 1), (-1, -1), (-1, 1), (1, -1), (1, 1), (0, -2), (0, 2)
)
OPP = tuple(DIRS.index((-a, -b)) for a, b in DIRS)


def relax_weight(k):
    return 1.0 / (1.4 + 0.6 * math.cos(math.pi * (2 * k + 1) / (2 * ROUNDS)))


def harmonic(a, b):
    return 2.0 * a * b / jnp.maximum(a + b, 1e-30)


def roll_x(v, s):
    return pltpu.roll(v.reshape(v.shape[0] // 8, 8, LANES), s % 8, 1).reshape(v.shape)


def roll_y(v, s):
    return pltpu.roll(v, s % LANES, 1)


def roll_z(v, s):
    return pltpu.roll(v, s % v.shape[0], 0)


def reduce_factors(low, high, roll):
    l, u, d = -low, -high, None
    parts = []
    for s in (1, 2, 4):
        if d is None:
            a, b, d = low, high, jnp.ones_like(low)
        else:
            rd = 1.0 / d
            a, b = -l * roll(rd, s), -u * roll(rd, -s)
        d = d + a * roll(u, s) + b * roll(l, -s)
        l, u = a * roll(l, s), b * roll(u, -s)
        parts += [a, b]
    return parts + [1.0 / d]


def reduce_x(r, f):
    a1, b1, a2, b2, c3, iv = f
    r = r + a1 * roll_x(r, 1) + b1 * roll_x(r, -1)
    r = r + a2 * roll_x(r, 2) + b2 * roll_x(r, -2)
    r = r + c3 * roll_x(r, 4)
    return r * iv


def reduce_y(r, f):
    a1, b1, a2, b2, a3, b3, iv = f
    r = r + a1 * roll_y(r, 1) + b1 * roll_y(r, -1)
    r = r + a2 * roll_y(r, 2) + b2 * roll_y(r, -2)
    r = r + a3 * roll_y(r, 4) + b3 * roll_y(r, -4)
    return r * iv


def col(x, planes=ROWS, first=0):
    return pl.ds(first * 8 + x, planes, stride=8)


def kernel(
    fac_h, fperm_h, pscale_h, src_h, p0_h, depth_h, out,
    fac, pscale, src, p0, fperm, depth, in_sem, gs, gr, c2r, outs, outr, ycf,
    zs, xs, ds, zr, xr, dr, mx, mzr, mxr, mdr, fzr, cs, cr,
    perm, pres, sper, spre, isrc, tgt, tside, e0, e1, e2, ub, corr,
    co, xf, yf, zf, gx, cx, sco, syf,
    i_send, i_recv, m_send, m_recv, f_send, f_recv, g_send, g_recv,
    c_send, c_recv, c2_send, c2_recv, a_send, a_recv,
):
    n_sub, n_grp = lax.axis_size("sub"), lax.axis_size("grp")
    sub, grp = lax.axis_index("sub"), lax.axis_index("grp")
    has_axis = {
        (-1, 0): sub > 0,
        (1, 0): sub < n_sub - 1,
        (0, -1): grp > 0,
        (0, 1): grp < n_grp - 1,
        (0, -2): grp > 1,
        (0, 2): grp < n_grp - 2,
    }
    has = []
    for dz, dx in DIRS:
        if dz and dx:
            has.append(jnp.logical_and(has_axis[(dz, 0)], has_axis[(0, dx)]))
        else:
            has.append(has_axis[(dz, dx)])

    def peer(d):
        return {"sub": sub + DIRS[d][0], "grp": grp + DIRS[d][1]}

    def remote(d, a, b, s_sem, r_sem):
        return pltpu.make_async_remote_copy(
            src_ref=a, dst_ref=b, send_sem=s_sem, recv_sem=r_sem,
            device_id=peer(d), device_id_type=MESH,
        )

    def exchange_start(dirs, make):
        for d in dirs:
            @pl.when(has[d])
            def _(d=d):
                make(d, OPP[d]).start()

    def exchange_wait(dirs, make):
        for d in dirs:
            @pl.when(has[d])
            def _(d=d):
                make(d, OPP[d]).wait_send()
                make(d, d).wait_recv()

    barrier = pltpu.get_barrier_semaphore()
    for d in range(len(DIRS)):
        @pl.when(has[d])
        def _(d=d):
            pl.semaphore_signal(barrier, inc=1, device_id=peer(d), device_id_type=MESH)

    loads = [
        pltpu.make_async_copy(a, b, in_sem.at[i])
        for i, (a, b) in enumerate((
            (fac_h, fac), (pscale_h, pscale), (p0_h, p0), (src_h, src),
            (fperm_h, fperm), (depth_h, depth),
        ))
    ]
    for load in loads:
        load.start()

    for d in range(len(DIRS)):
        @pl.when(jnp.logical_not(has[d]))
        def _(d=d):
            if d < 2:
                zr[d] = jnp.zeros(zr.shape[1:], jnp.float32)
                mzr[d] = jnp.zeros(mzr.shape[1:], jnp.float32)
                fzr[d] = jnp.zeros(fzr.shape[1:], jnp.float32)
            elif d < 4:
                xr[d - 2] = jnp.zeros(xr.shape[1:], jnp.float32)
                mxr[d - 2] = jnp.zeros(mxr.shape[1:], jnp.float32)
                gr[d - 2] = jnp.zeros(gr.shape[1:], jnp.float32)
                for ph in range(cr.shape[0]):
                    cr[ph, d - 2] = jnp.zeros(cr.shape[2:], jnp.float32)
                    outr[ph, d - 2] = jnp.zeros(outr.shape[2:], jnp.float32)
            elif d < 8:
                dr[d - 4] = jnp.zeros(dr.shape[1:], jnp.float32)
                mdr[d - 4] = jnp.zeros(mdr.shape[1:], jnp.float32)
            else:
                for ph in range(c2r.shape[0]):
                    c2r[ph, d - 8] = jnp.zeros(c2r.shape[2:], jnp.float32)

    for load in loads:
        load.wait()

    kinds = fac[...]
    own = jnp.zeros(kinds.shape, jnp.float32)
    for kind in range(FACIES):
        own = jnp.where(kinds == kind, fperm[kind], own)
    own = (own * pscale[...]).reshape(OWN * 8, LANES)
    perm[pl.ds(40, OWN * 8)] = own
    pres[pl.ds(40, OWN * 8)] = p0[...].reshape(OWN * 8, LANES)
    isrc[pl.ds(32, OWN * 8)] = src[...].reshape(OWN * 8, LANES)
    for s in range(2):
        at = 5 if s == 0 else 16
        zs[s, pl.ds(0, 40)] = perm[pl.ds(at * 8, 40)]
        zs[s, pl.ds(40, 40)] = pres[pl.ds(at * 8, 40)]
        zs[s, pl.ds(80, 32)] = isrc[pl.ds(32 if s == 0 else 128, 32)]
        near, far = (0, 1) if s == 0 else (7, 6)
        kn, kf, pn = perm[col(near, 16, 5)], perm[col(far, 16, 5)], pres[col(near, 16, 5)]
        xs[s, pl.ds(0, 16)] = kn
        xs[s, pl.ds(16, 16)] = kf
        xs[s, pl.ds(32, 16)] = pn
        for z in range(2):
            at_rows = 5 if z == 0 else 13
            ds[2 * z + s, pl.ds(0, 8)] = perm[col(near, 8, at_rows)]
            ds[2 * z + s, pl.ds(8, 8)] = perm[col(far, 8, at_rows)]
            ds[2 * z + s, pl.ds(16, 8)] = pres[col(near, 8, at_rows)]

    def init_copy(d, slot):
        if d < 2:
            a, b = zs.at[d], zr.at[slot]
        elif d < 4:
            a, b = xs.at[d - 2], xr.at[slot - 2]
        else:
            a, b = ds.at[d - 4], dr.at[slot - 4]
        return remote(d, a, b, i_send.at[d], i_recv.at[slot])

    pl.semaphore_wait(barrier, sum(jnp.where(h, 1, 0) for h in has))
    exchange_start(range(8), init_copy)

    low = jnp.where(sub > 0, depth[jnp.maximum(sub - 1, 0)], 0)
    high = jnp.where(sub < n_sub - 1, depth[jnp.minimum(sub, n_sub - 2)], 0)

    def active(rows):
        inside = (rows >= OV - low) & (rows < OV + OWN + high)
        return jnp.where(inside, 1.0, 0.0)

    def rows_of(c):
        return lax.broadcasted_iota(jnp.int32, (8, 8, LANES), 0).reshape(CH, LANES) + 8 * c

    lane = lax.broadcasted_iota(jnp.int32, (CH, LANES), 1)
    lane2 = lax.broadcasted_iota(jnp.int32, (ROWS, LANES), 1)
    row2 = lax.broadcasted_iota(jnp.int32, (ROWS, LANES), 0)
    subl = lax.broadcasted_iota(jnp.int32, (8, 8, LANES), 1).reshape(CH, LANES)
    zeros_plane = jnp.zeros((8, LANES), jnp.float32)
    for e in (e0, e1, e2):
        e[pl.ds(0, 8)] = zeros_plane
        e[pl.ds((ROWS + 1) * 8, 8)] = zeros_plane

    exchange_wait(range(8), init_copy)

    perm[pl.ds(0, 40)] = zr[0, pl.ds(0, 40)]
    pres[pl.ds(0, 40)] = zr[0, pl.ds(40, 40)]
    isrc[pl.ds(0, 32)] = zr[0, pl.ds(80, 32)]
    perm[pl.ds(168, 40)] = zr[1, pl.ds(0, 40)]
    pres[pl.ds(168, 40)] = zr[1, pl.ds(40, 40)]
    isrc[pl.ds(160, 32)] = zr[1, pl.ds(80, 32)]
    for s in range(2):
        for f in range(2):
            sper[s, f, pl.ds(5, 16)] = xr[s, pl.ds(16 * f, 16)]
            sper[s, f, pl.ds(0, 5)] = dr[s, pl.ds(8 * f + 3, 5)]
            sper[s, f, pl.ds(21, 5)] = dr[2 + s, pl.ds(8 * f, 5)]
        spre[s, pl.ds(4, 16)] = xr[s, pl.ds(32, 16)]
        spre[s, pl.ds(0, 4)] = dr[s, pl.ds(20, 4)]
        spre[s, pl.ds(20, 4)] = dr[2 + s, pl.ds(16, 4)]
        ub[col(7 * s)] = sper[s, 0, pl.ds(1, ROWS)]

    for c in range(CHUNKS):
        here = pl.ds(c * CH, CH)
        mid = perm[pl.ds((c * 8 + 1) * 8, CH)]
        edge = ub[here]
        fb = harmonic(perm[pl.ds(c * CH, CH)], mid)
        fa = harmonic(mid, perm[pl.ds((c * 8 + 2) * 8, CH)])
        fl = harmonic(jnp.where(subl == 0, edge, roll_x(mid, 1)), mid)
        fr = harmonic(mid, jnp.where(subl == 7, edge, roll_x(mid, -1)))
        ff = harmonic(jnp.where(lane == 0, 0.0, roll_y(mid, 1)), mid)
        fk = harmonic(mid, jnp.where(lane == LANES - 1, 0.0, roll_y(mid, -1)))
        act = active(rows_of(c))
        inv = act / (STORE + fb + fa + fl + fr + ff + fk)
        fl, fr = fl * inv, fr * inv
        ub[here] = jnp.where(subl == 0, fl, fr)
        fl, fr = jnp.where(subl == 0, 0.0, fl), jnp.where(subl == 7, 0.0, fr)
        fb, fa, ff, fk = fb * inv, fa * inv, ff * inv, fk * inv
        for i, f in enumerate((fb, fa, fl, fr, ff, fk)):
            co[i, here] = f
        isrc[here] = isrc[here] * inv
        a1, b1, a2, b2, a3, b3, iv = reduce_factors(fl, fr, roll_x)
        for i, f in enumerate((a2, b2, a3 + b3, iv)):
            xf[i, here] = f
    for s in range(2):
        cx[s] = ub[col(7 * s)]

    def xfac(here):
        return [co[2, here], co[3, here]] + [xf[i, here] for i in range(4)]

    for c in range(CHUNKS):
        gx[0, pl.ds(c * CH, CH)] = ub[pl.ds(c * CH, CH)]
        ub[pl.ds(c * CH, CH)] = jnp.zeros((CH, LANES), jnp.float32)

    def answer_copy(d, slot):
        return remote(
            d, gs.at[d - 2], gr.at[slot - 2], g_send.at[d - 2], g_recv.at[slot - 2]
        )

    def rest_of_setup():
        for c in range(CHUNKS):
            here = pl.ds(c * CH, CH)
            fb, fa, ff, fk = (co[i, here] for i in (0, 1, 4, 5))
            fy = reduce_factors(
                jnp.where(lane % BL == 0, 0.0, ff), jnp.where(lane % BL == BL - 1, 0.0, fk), roll_y
            )
            for i, f in enumerate(fy):
                yf[i, here] = f
            lz = -fb * active(rows_of(c) - 1)
            uz = -fa * active(rows_of(c) + 1)
            d = None
            for i in range(BL):
                at = pl.ds(c * CH + i * 8, 8)
                part = slice(i * 8, i * 8 + 8)
                if i == 0:
                    m, d = zeros_plane, jnp.ones((8, LANES), jnp.float32)
                else:
                    m = lz[part] / d
                    d = 1.0 - m * uz[(i - 1) * 8 : i * 8]
                zf[0, at] = m
                zf[1, at] = 1.0 / d
                zf[2, at] = uz[part] / d
        for c in range(CHUNKS):
            here = pl.ds(c * CH, CH)
            edge, f = gx[0, here], xfac(here)
            for s in range(2):
                gx[s, here] = reduce_x(jnp.where(subl == 7 * s, edge, 0.0), f)
        for s in range(2):
            near, far = (0, 1) if s == 0 else (7, 6)
            for i in range(2):
                gs[s, pl.ds(2 * i * ROWS, ROWS)] = gx[i, col(near)]
                gs[s, pl.ds((2 * i + 1) * ROWS, ROWS)] = gx[i, col(far)]

        exchange_start((2, 3), answer_copy)

        for s in range(2):
            for i in range(7):
                ycf[s, i] = yf[i, col(7 * s)]

        for s in range(2):
            mid = sper[s, 0, pl.ds(1, ROWS)]
            fb = harmonic(sper[s, 0, pl.ds(0, ROWS)], mid)
            fa = harmonic(mid, sper[s, 0, pl.ds(2, ROWS)])
            fx = harmonic(mid, sper[s, 1, pl.ds(1, ROWS)])
            fo = harmonic(mid, perm[col(7 * s, ROWS, 1)])
            ff = harmonic(jnp.where(lane2 == 0, 0.0, roll_y(mid, 1)), mid)
            fk = harmonic(mid, jnp.where(lane2 == LANES - 1, 0.0, roll_y(mid, -1)))
            inv = active(row2) / (STORE + fb + fa + fx + fo + ff + fk)
            fb = jnp.where(row2 == 0, 0.0, fb * inv)
            fa = jnp.where(row2 == ROWS - 1, 0.0, fa * inv)
            ff, fk = ff * inv, fk * inv
            for i, f in enumerate((fb, fa, fx * inv, fo * inv, ff, fk)):
                sco[s, i] = f
            fy = reduce_factors(
                jnp.where(lane2 % BL == 0, 0.0, ff), jnp.where(lane2 % BL == BL - 1, 0.0, fk), roll_y
            )
            for i, f in enumerate(fy):
                syf[s, i] = f

    def update(t, e, c, scale=None):
        here = pl.ds(c * CH, CH)
        v = e[pl.ds((c * 8 + 1) * 8, CH)]
        u = t[here] - (v if scale is None else v * scale)
        u = u + co[0, here] * e[pl.ds(c * CH, CH)] + co[1, here] * e[pl.ds((c * 8 + 2) * 8, CH)]
        u = u + co[2, here] * roll_x(v, 1) + co[3, here] * roll_x(v, -1)
        return v, u + co[4, here] * roll_y(v, 1) + co[5, here] * roll_y(v, -1)

    def col_copy(ph, rows):
        def make(d, slot):
            return remote(
                d, cs.at[ph, d - 2, pl.ds(0, rows)], cr.at[ph, slot - 2, pl.ds(0, rows)],
                c_send.at[ph, d - 2], c_recv.at[ph, slot - 2],
            )
        return make

    def solved_copy(ph):
        def make(d, slot):
            if d < 4:
                return remote(
                    d, outs.at[ph, d - 2], outr.at[ph, slot - 2],
                    a_send.at[ph, d - 2], a_recv.at[ph, slot - 2],
                )
            return remote(
                d, outs.at[ph, d - 8], c2r.at[ph, slot - 8],
                c2_send.at[ph, d - 8], c2_recv.at[ph, slot - 8],
            )
        return make

    def one_round(outer, k):
        first = isinstance(k, int)
        ph = outer * ROUNDS + k
        om = relax_weight(0)
        if not first:
            for i in range(1, ROUNDS):
                om = jnp.where(k == i, jnp.float32(relax_weight(i)), om)
        for c in range(CHUNKS):
            here = pl.ds(c * CH, CH)
            if first:
                e1[pl.ds((c * 8 + 1) * 8, CH)] = om * reduce_x(tgt[here], xfac(here))
            else:
                v, u = update(tgt, e0, c)
                e1[pl.ds((c * 8 + 1) * 8, CH)] = v + om * reduce_x(u, xfac(here))
        for s in range(2):
            near, far = (0, 1) if s == 0 else (7, 6)
            cs[ph, s, pl.ds(0, ROWS)] = e1[col(near, ROWS, 1)]
            cs[ph, s, pl.ds(ROWS, ROWS)] = e1[col(far, ROWS, 1)]
            if first:
                cs[ph, s, pl.ds(2 * ROWS, ROWS)] = tgt[col(near)]
        make = col_copy(ph, (3 if first else 2) * ROWS)
        exchange_start((2, 3), make)
        if first and outer == 0:
            rest_of_setup()
        if not first:
            exchange_wait((2, 3, 8, 9), solved_copy(ph))
            for z in range(ROWS):
                at, here = pl.ds((z + 1) * 8, 8), pl.ds(z * 8, 8)
                left = jnp.broadcast_to(outr[ph, 0, pl.ds(z, 1)], (8, LANES))
                right = jnp.broadcast_to(outr[ph, 1, pl.ds(z, 1)], (8, LANES))
                e1[at] = e1[at] + om * (gx[0, here] * left + gx[1, here] * right)
        for c in range(CHUNKS):
            here = pl.ds(c * CH, CH)
            v, u = update(tgt, e1, c)
            e2[pl.ds((c * 8 + 1) * 8, CH)] = v + om * reduce_y(u, [yf[i, here] for i in range(7)])
        exchange_wait((2, 3), make)
        for s in range(2):
            near, far = cr[ph, s, pl.ds(0, ROWS)], cr[ph, s, pl.ds(ROWS, ROWS)]
            if first:
                tside[s] = cr[ph, s, pl.ds(2 * ROWS, ROWS)]
            else:
                beyond, inner = c2r[ph, s], e0[col(7 * s, ROWS, 1)]
                left, right = (beyond, inner) if s == 0 else (inner, beyond)
                g = [gr[s, pl.ds(i * ROWS, ROWS)] for i in range(4)]
                near = near + om * (g[0] * left + g[2] * right)
                far = far + om * (g[1] * left + g[3] * right)
            u = tside[s] - near
            u = u + sco[s, 0] * roll_z(near, 1) + sco[s, 1] * roll_z(near, -1)
            u = u + sco[s, 2] * far + sco[s, 3] * e1[col(7 * s, ROWS, 1)]
            u = u + sco[s, 4] * roll_y(near, 1) + sco[s, 5] * roll_y(near, -1)
            beside = near + om * reduce_y(u, [syf[s, i] for i in range(7)])
            ub[col(7 * s)] = cx[s] * beside
            at = col(7 * s, ROWS, 1)
            e2[at] = e2[at] + om * reduce_y(cx[s] * near, [ycf[s, i] for i in range(7)])
        for c in range(CHUNKS):
            v, u = update(tgt, e2, c)
            u = u + ub[pl.ds(c * CH, CH)]
            fw, prev = [], None
            for i in range(BL):
                at, r = pl.ds(c * CH + i * 8, 8), u[i * 8 : i * 8 + 8]
                prev = r if i == 0 else r - zf[0, at] * prev
                fw.append(prev)
            nxt = None
            for i in range(BL - 1, -1, -1):
                at = pl.ds(c * CH + i * 8, 8)
                nxt = fw[i] * zf[1, at] if nxt is None else fw[i] * zf[1, at] - zf[2, at] * nxt
                e0[pl.ds((c * 8 + i + 1) * 8, 8)] = v[i * 8 : i * 8 + 8] + om * nxt

        def send_next():
            for s in range(2):
                outs[ph + 1, s] = e0[col(7 * s, ROWS, 1)]
            exchange_start((2, 3, 8, 9), solved_copy(ph + 1))

        if first:
            send_next()
        else:
            pl.when(k < ROUNDS - 1)(send_next)

    def mid_copy(d, slot):
        if d < 2:
            a, b = corr.at[pl.ds(0 if d == 0 else 120, 72)], mzr.at[slot]
        elif d < 4:
            a, b = mx.at[d - 2], mxr.at[slot - 2]
        else:
            z, s = divmod(d - 4, 2)
            a, b = mx.at[s, pl.ds(16 * z, 8)], mdr.at[slot - 4]
        return remote(d, a, b, m_send.at[d], m_recv.at[slot])

    def end_copy(d, slot):
        a = corr.at[pl.ds(0 if d == 0 else 160, 32)]
        return remote(d, a, fzr.at[slot], f_send.at[d], f_recv.at[slot])

    for outer in range(OUTER):
        for s in range(2):
            ub[col(7 * s)] = cx[s] * spre[s]
        for c in range(CHUNKS):
            u = update(isrc, pres, c, active(rows_of(c)))[1]
            tgt[pl.ds(c * CH, CH)] = u + ub[pl.ds(c * CH, CH)]
        one_round(outer, 0)
        if outer == 0:
            exchange_wait((2, 3), answer_copy)

        def step(k, carry, outer=outer):
            one_round(outer, k)
            return carry

        lax.fori_loop(1, ROUNDS, step, 0)
        for c in range(CHUNKS):
            rows = rows_of(c)
            band = (rows < OV + low) | (rows >= OV + OWN - high)
            w = active(rows) * jnp.where(band, 0.5, 1.0)
            corr[pl.ds(c * CH, CH)] = w * e0[pl.ds((c * 8 + 1) * 8, CH)]
        if outer == 0:
            for s in range(2):
                mx[s] = corr[col(7 * s)]
            exchange_start(range(8), mid_copy)
            pres[pl.ds(8, ROWS * 8)] = pres[pl.ds(8, ROWS * 8)] + corr[...]
            exchange_wait(range(8), mid_copy)
            for z in range(2):
                at = pl.ds(0 if z == 0 else 17 * 8, 72)
                pres[at] = pres[at] + mzr[z]
            for s in range(2):
                spre[s] = spre[s] + mxr[s]
                for z in range(2):
                    at = pl.ds(16 * z, 8)
                    spre[s, at] = spre[s, at] + mdr[2 * z + s]
        else:
            exchange_start((0, 1), end_copy)
            pres[pl.ds(8, ROWS * 8)] = pres[pl.ds(8, ROWS * 8)] + corr[...]
            exchange_wait((0, 1), end_copy)
            for z in range(2):
                at = pl.ds(40 if z == 0 else 17 * 8, 32)
                pres[at] = pres[at] + fzr[z]
    out[...] = pres[pl.ds(40, OWN * 8)].reshape(OWN, 8, LANES)


def on_device(facies, facies_perm, perm_scale, source, pressure_start, intersection_depth):
    assert source.shape == (OWN, 8, LANES)
    f32 = jnp.float32

    def buf(*shape):
        return pltpu.VMEM(shape, f32)

    field, wide = (ROWS * 8, LANES), (WIDE * 8, LANES)
    phases, own, dma = OUTER * ROUNDS, source.shape, pltpu.SemaphoreType.DMA
    scratch = [
        pltpu.VMEM(own, jnp.int32), buf(*own), buf(*own), buf(*own),
        pltpu.SMEM(facies_perm.shape, f32), pltpu.SMEM(intersection_depth.shape, jnp.int32),
        dma((6,)), buf(2, 4 * ROWS, LANES), buf(2, 4 * ROWS, LANES),
        *[buf(phases, 2, ROWS, LANES)] * 3, buf(2, 7, ROWS, LANES),
        buf(2, 112, LANES), buf(2, 48, LANES), buf(4, 24, LANES),
        buf(2, 112, LANES), buf(2, 48, LANES), buf(4, 24, LANES),
        buf(2, ROWS, LANES), buf(2, 72, LANES), buf(2, ROWS, LANES), buf(4, 8, LANES),
        buf(2, 32, LANES), buf(phases, 2, 3 * ROWS, LANES), buf(phases, 2, 3 * ROWS, LANES),
        buf(*wide), buf(*wide), buf(2, 2, 32, LANES), buf(2, ROWS, LANES),
        buf(*field), buf(*field), buf(2, ROWS, LANES),
        buf(*wide), buf(*wide), buf(*wide), buf(*field), buf(*field),
        buf(6, *field), buf(4, *field), buf(7, *field), buf(3, *field),
        buf(2, *field), buf(2, ROWS, LANES), buf(2, 6, ROWS, LANES), buf(2, 7, ROWS, LANES),
    ]
    sems = [dma((n,)) for n in (8, 8, 8, 8, 2, 2, 2, 2)]
    sems += [dma((phases, 2)) for _ in range(6)]
    return pl.pallas_call(
        kernel,
        out_shape=jax.ShapeDtypeStruct(source.shape, f32),
        in_specs=[pl.BlockSpec(memory_space=pltpu.HBM)] * 6,
        out_specs=pl.BlockSpec(memory_space=pltpu.VMEM),
        scratch_shapes=scratch + sems,
        compiler_params=pltpu.CompilerParams(
            collective_id=0, has_side_effects=True, vmem_limit_bytes=60 * 1024 * 1024
        ),
        name="schwarz",
    )(facies, facies_perm, perm_scale, source, pressure_start, intersection_depth)


def solution(mesh):
    return jax.shard_map(
        on_device,
        mesh=mesh,
        in_specs=(
            P("sub", "grp", None),
            P(),
            P("sub", "grp", None),
            P("sub", "grp", None),
            P("sub", "grp", None),
            P(),
        ),
        out_specs=P("sub", "grp", None),
        check_vma=False,
    )
```

```python
import functools
import math

import jax
import jax.numpy as jnp
from jax import lax
from jax.experimental import pallas as pl
from jax.experimental.pallas import tpu as pltpu
from jax.sharding import PartitionSpec as P

OV = 4
BL = 8
ROUNDS = 4
OUTER = 2
FACIES = 8
STORE = 0.02
MESH = pl.DeviceIdType.MESH

OWN = 16
ROWS = OWN + 2 * OV
WIDE = ROWS + 2
LANES = 128
CHUNKS = ROWS // BL
CH = BL * 8
PIECE = ROWS * 8

DIRS = (
    (-1, 0), (1, 0), (0, -1), (0, 1), (-1, -1), (-1, 1), (1, -1), (1, 1), (0, -2), (0, 2)
)
OPP = tuple(DIRS.index((-a, -b)) for a, b in DIRS)


def relax_weight(k):
    return 1.0 / (1.4 + 0.6 * math.cos(math.pi * (2 * k + 1) / (2 * ROUNDS)))


def harmonic(a, b):
    return 2.0 * a * b / jnp.maximum(a + b, 1e-30)


def roll_x(v, s):
    return pltpu.roll(v.reshape(v.shape[0] // 8, 8, LANES), s % 8, 1).reshape(v.shape)


def roll_y(v, s):
    return pltpu.roll(v, s % LANES, 1)


def roll_z(v, s):
    return pltpu.roll(v, s % v.shape[0], 0)


def reduce_factors(low, high, roll):
    l, u, d = -low, -high, None
    parts = []
    for s in (1, 2, 4):
        if d is None:
            a, b, d = low, high, jnp.ones_like(low)
        else:
            rd = 1.0 / d
            a, b = -l * roll(rd, s), -u * roll(rd, -s)
        d = d + a * roll(u, s) + b * roll(l, -s)
        l, u = a * roll(l, s), b * roll(u, -s)
        parts += [a, b]
    return parts + [1.0 / d]


def reduce_x(r, f):
    a1, b1, a2, b2, c3, iv = f
    r = r + a1 * roll_x(r, 1) + b1 * roll_x(r, -1)
    r = r + a2 * roll_x(r, 2) + b2 * roll_x(r, -2)
    r = r + c3 * roll_x(r, 4)
    return r * iv


def reduce_y(r, f):
    a1, b1, a2, b2, a3, b3, iv = f
    r = r + a1 * roll_y(r, 1) + b1 * roll_y(r, -1)
    r = r + a2 * roll_y(r, 2) + b2 * roll_y(r, -2)
    r = r + a3 * roll_y(r, 4) + b3 * roll_y(r, -4)
    return r * iv


def col(x, planes=ROWS, first=0):
    return pl.ds(first * 8 + x, planes, stride=8)


def kernel(
    fac_h, fperm_h, pscale_h, src_h, p0_h, depth_h, out,
    fac, pscale, src, p0, fperm, depth, in_sem, gs, gr, c2r, outs, outr, ycf,
    zs, xs, ds, zr, xr, dr, mx, mzr, mxr, mdr, fzr, cs, cr,
    perm, pres, sper, spre, isrc, tgt, tside, e0, e1, e2, ub, corr,
    co, xf, yf, zf, gx, cx, sco, syf,
    i_send, i_recv, m_send, m_recv, f_send, f_recv, g_send, g_recv,
    c_send, c_recv, c2_send, c2_recv, a_send, a_recv,
):
    n_sub, n_grp = lax.axis_size("sub"), lax.axis_size("grp")
    sub, grp = lax.axis_index("sub"), lax.axis_index("grp")
    has_axis = {
        (-1, 0): sub > 0,
        (1, 0): sub < n_sub - 1,
        (0, -1): grp > 0,
        (0, 1): grp < n_grp - 1,
        (0, -2): grp > 1,
        (0, 2): grp < n_grp - 2,
    }
    has = []
    for dz, dx in DIRS:
        if dz and dx:
            has.append(jnp.logical_and(has_axis[(dz, 0)], has_axis[(0, dx)]))
        else:
            has.append(has_axis[(dz, dx)])

    def peer(d):
        return {"sub": sub + DIRS[d][0], "grp": grp + DIRS[d][1]}

    def remote(d, a, b, s_sem, r_sem):
        return pltpu.make_async_remote_copy(
            src_ref=a, dst_ref=b, send_sem=s_sem, recv_sem=r_sem,
            device_id=peer(d), device_id_type=MESH,
        )

    def exchange_start(dirs, make):
        for d in dirs:
            @pl.when(has[d])
            def _(d=d):
                make(d, OPP[d]).start()

    def exchange_wait(dirs, make):
        for d in dirs:
            @pl.when(has[d])
            def _(d=d):
                make(d, OPP[d]).wait_send()
                make(d, d).wait_recv()

    barrier = pltpu.get_barrier_semaphore()
    for d in range(len(DIRS)):
        @pl.when(has[d])
        def _(d=d):
            pl.semaphore_signal(barrier, inc=1, device_id=peer(d), device_id_type=MESH)

    loads = [
        pltpu.make_async_copy(a, b, in_sem.at[i])
        for i, (a, b) in enumerate((
            (fac_h, fac), (pscale_h, pscale), (p0_h, p0), (src_h, src),
            (fperm_h, fperm), (depth_h, depth),
        ))
    ]
    for load in loads:
        load.start()

    for d in range(len(DIRS)):
        @pl.when(jnp.logical_not(has[d]))
        def _(d=d):
            if d < 2:
                zr[d] = jnp.zeros(zr.shape[1:], jnp.float32)
                mzr[d] = jnp.zeros(mzr.shape[1:], jnp.float32)
                fzr[d] = jnp.zeros(fzr.shape[1:], jnp.float32)
            elif d < 4:
                xr[d - 2] = jnp.zeros(xr.shape[1:], jnp.float32)
                mxr[d - 2] = jnp.zeros(mxr.shape[1:], jnp.float32)
                gr[d - 2] = jnp.zeros(gr.shape[1:], jnp.float32)
                for ph in range(cr.shape[0]):
                    cr[ph, d - 2] = jnp.zeros(cr.shape[2:], jnp.float32)
                    outr[ph, d - 2] = jnp.zeros(outr.shape[2:], jnp.float32)
            elif d < 8:
                dr[d - 4] = jnp.zeros(dr.shape[1:], jnp.float32)
                mdr[d - 4] = jnp.zeros(mdr.shape[1:], jnp.float32)
            else:
                for ph in range(c2r.shape[0]):
                    c2r[ph, d - 8] = jnp.zeros(c2r.shape[2:], jnp.float32)

    for load in loads:
        load.wait()

    kinds = fac[...]
    own = jnp.zeros(kinds.shape, jnp.float32)
    for kind in range(FACIES):
        own = jnp.where(kinds == kind, fperm[kind], own)
    own = (own * pscale[...]).reshape(OWN * 8, LANES)
    perm[pl.ds(40, OWN * 8)] = own
    pres[pl.ds(40, OWN * 8)] = p0[...].reshape(OWN * 8, LANES)
    isrc[pl.ds(32, OWN * 8)] = src[...].reshape(OWN * 8, LANES)
    for s in range(2):
        at = 5 if s == 0 else 16
        zs[s, pl.ds(0, 40)] = perm[pl.ds(at * 8, 40)]
        zs[s, pl.ds(40, 40)] = pres[pl.ds(at * 8, 40)]
        zs[s, pl.ds(80, 32)] = isrc[pl.ds(32 if s == 0 else 128, 32)]
        near, far = (0, 1) if s == 0 else (7, 6)
        kn, kf, pn = perm[col(near, 16, 5)], perm[col(far, 16, 5)], pres[col(near, 16, 5)]
        xs[s, pl.ds(0, 16)] = kn
        xs[s, pl.ds(16, 16)] = kf
        xs[s, pl.ds(32, 16)] = pn
        for z in range(2):
            at_rows = 5 if z == 0 else 13
            ds[2 * z + s, pl.ds(0, 8)] = perm[col(near, 8, at_rows)]
            ds[2 * z + s, pl.ds(8, 8)] = perm[col(far, 8, at_rows)]
            ds[2 * z + s, pl.ds(16, 8)] = pres[col(near, 8, at_rows)]

    def init_copy(d, slot):
        if d < 2:
            a, b = zs.at[d], zr.at[slot]
        elif d < 4:
            a, b = xs.at[d - 2], xr.at[slot - 2]
        else:
            a, b = ds.at[d - 4], dr.at[slot - 4]
        return remote(d, a, b, i_send.at[d], i_recv.at[slot])

    pl.semaphore_wait(barrier, sum(jnp.where(h, 1, 0) for h in has))
    exchange_start(range(8), init_copy)

    low = jnp.where(sub > 0, depth[jnp.maximum(sub - 1, 0)], 0)
    high = jnp.where(sub < n_sub - 1, depth[jnp.minimum(sub, n_sub - 2)], 0)

    def active(rows):
        inside = (rows >= OV - low) & (rows < OV + OWN + high)
        return jnp.where(inside, 1.0, 0.0)

    def rows_of(c):
        return lax.broadcasted_iota(jnp.int32, (8, 8, LANES), 0).reshape(CH, LANES) + 8 * c

    lane = lax.broadcasted_iota(jnp.int32, (CH, LANES), 1)
    lane2 = lax.broadcasted_iota(jnp.int32, (ROWS, LANES), 1)
    row2 = lax.broadcasted_iota(jnp.int32, (ROWS, LANES), 0)
    subl = lax.broadcasted_iota(jnp.int32, (8, 8, LANES), 1).reshape(CH, LANES)
    zeros_plane = jnp.zeros((8, LANES), jnp.float32)
    for e in (e0, e1, e2):
        e[pl.ds(0, 8)] = zeros_plane
        e[pl.ds((ROWS + 1) * 8, 8)] = zeros_plane

    exchange_wait(range(8), init_copy)

    perm[pl.ds(0, 40)] = zr[0, pl.ds(0, 40)]
    pres[pl.ds(0, 40)] = zr[0, pl.ds(40, 40)]
    isrc[pl.ds(0, 32)] = zr[0, pl.ds(80, 32)]
    perm[pl.ds(168, 40)] = zr[1, pl.ds(0, 40)]
    pres[pl.ds(168, 40)] = zr[1, pl.ds(40, 40)]
    isrc[pl.ds(160, 32)] = zr[1, pl.ds(80, 32)]
    for s in range(2):
        for f in range(2):
            sper[s, f, pl.ds(5, 16)] = xr[s, pl.ds(16 * f, 16)]
            sper[s, f, pl.ds(0, 5)] = dr[s, pl.ds(8 * f + 3, 5)]
            sper[s, f, pl.ds(21, 5)] = dr[2 + s, pl.ds(8 * f, 5)]
        spre[s, pl.ds(4, 16)] = xr[s, pl.ds(32, 16)]
        spre[s, pl.ds(0, 4)] = dr[s, pl.ds(20, 4)]
        spre[s, pl.ds(20, 4)] = dr[2 + s, pl.ds(16, 4)]
        ub[col(7 * s)] = sper[s, 0, pl.ds(1, ROWS)]

    for c in range(CHUNKS):
        here = pl.ds(c * CH, CH)
        mid = perm[pl.ds((c * 8 + 1) * 8, CH)]
        edge = ub[here]
        fb = harmonic(perm[pl.ds(c * CH, CH)], mid)
        fa = harmonic(mid, perm[pl.ds((c * 8 + 2) * 8, CH)])
        fl = harmonic(jnp.where(subl == 0, edge, roll_x(mid, 1)), mid)
        fr = harmonic(mid, jnp.where(subl == 7, edge, roll_x(mid, -1)))
        ff = harmonic(jnp.where(lane == 0, 0.0, roll_y(mid, 1)), mid)
        fk = harmonic(mid, jnp.where(lane == LANES - 1, 0.0, roll_y(mid, -1)))
        act = active(rows_of(c))
        inv = act / (STORE + fb + fa + fl + fr + ff + fk)
        fl, fr = fl * inv, fr * inv
        ub[here] = jnp.where(subl == 0, fl, fr)
        fl, fr = jnp.where(subl == 0, 0.0, fl), jnp.where(subl == 7, 0.0, fr)
        fb, fa, ff, fk = fb * inv, fa * inv, ff * inv, fk * inv
        for i, f in enumerate((fb, fa, fl, fr, ff, fk)):
            co[i, here] = f
        isrc[here] = isrc[here] * inv
        a1, b1, a2, b2, a3, b3, iv = reduce_factors(fl, fr, roll_x)
        for i, f in enumerate((a2, b2, a3 + b3, iv)):
            xf[i, here] = f
    for s in range(2):
        cx[s] = ub[col(7 * s)]

    def xfac(here):
        return [co[2, here], co[3, here]] + [xf[i, here] for i in range(4)]

    for c in range(CHUNKS):
        gx[0, pl.ds(c * CH, CH)] = ub[pl.ds(c * CH, CH)]
        ub[pl.ds(c * CH, CH)] = jnp.zeros((CH, LANES), jnp.float32)

    def answer_copy(d, slot):
        return remote(
            d, gs.at[d - 2], gr.at[slot - 2], g_send.at[d - 2], g_recv.at[slot - 2]
        )

    def rest_of_setup():
        for c in range(CHUNKS):
            here = pl.ds(c * CH, CH)
            fb, fa, ff, fk = (co[i, here] for i in (0, 1, 4, 5))
            fy = reduce_factors(
                jnp.where(lane % BL == 0, 0.0, ff), jnp.where(lane % BL == BL - 1, 0.0, fk), roll_y
            )
            for i, f in enumerate(fy):
                yf[i, here] = f
            lz = -fb * active(rows_of(c) - 1)
            uz = -fa * active(rows_of(c) + 1)
            d = None
            for i in range(BL):
                at = pl.ds(c * CH + i * 8, 8)
                part = slice(i * 8, i * 8 + 8)
                if i == 0:
                    m, d = zeros_plane, jnp.ones((8, LANES), jnp.float32)
                else:
                    m = lz[part] / d
                    d = 1.0 - m * uz[(i - 1) * 8 : i * 8]
                zf[0, at] = m
                zf[1, at] = 1.0 / d
                zf[2, at] = uz[part] / d
        for c in range(CHUNKS):
            here = pl.ds(c * CH, CH)
            edge, f = gx[0, here], xfac(here)
            for s in range(2):
                gx[s, here] = reduce_x(jnp.where(subl == 7 * s, edge, 0.0), f)
        for s in range(2):
            near, far = (0, 1) if s == 0 else (7, 6)
            for i in range(2):
                gs[s, pl.ds(2 * i * ROWS, ROWS)] = gx[i, col(near)]
                gs[s, pl.ds((2 * i + 1) * ROWS, ROWS)] = gx[i, col(far)]

        exchange_start((2, 3), answer_copy)

        for s in range(2):
            for i in range(7):
                ycf[s, i] = yf[i, col(7 * s)]

        for s in range(2):
            mid = sper[s, 0, pl.ds(1, ROWS)]
            fb = harmonic(sper[s, 0, pl.ds(0, ROWS)], mid)
            fa = harmonic(mid, sper[s, 0, pl.ds(2, ROWS)])
            fx = harmonic(mid, sper[s, 1, pl.ds(1, ROWS)])
            fo = harmonic(mid, perm[col(7 * s, ROWS, 1)])
            ff = harmonic(jnp.where(lane2 == 0, 0.0, roll_y(mid, 1)), mid)
            fk = harmonic(mid, jnp.where(lane2 == LANES - 1, 0.0, roll_y(mid, -1)))
            inv = active(row2) / (STORE + fb + fa + fx + fo + ff + fk)
            fb = jnp.where(row2 == 0, 0.0, fb * inv)
            fa = jnp.where(row2 == ROWS - 1, 0.0, fa * inv)
            ff, fk = ff * inv, fk * inv
            for i, f in enumerate((fb, fa, fx * inv, fo * inv, ff, fk)):
                sco[s, i] = f
            fy = reduce_factors(
                jnp.where(lane2 % BL == 0, 0.0, ff), jnp.where(lane2 % BL == BL - 1, 0.0, fk), roll_y
            )
            for i, f in enumerate(fy):
                syf[s, i] = f

    def update(t, e, at, scale=None):
        here = pl.ds(at, PIECE)
        v = e[pl.ds(at + 8, PIECE)]
        u = t[here] - (v if scale is None else v * scale)
        u = u + co[0, here] * e[here] + co[1, here] * e[pl.ds(at + 16, PIECE)]
        u = u + co[2, here] * roll_x(v, 1) + co[3, here] * roll_x(v, -1)
        return v, u + co[4, here] * roll_y(v, 1) + co[5, here] * roll_y(v, -1)

    def col_copy(ph, rows):
        def make(d, slot):
            return remote(
                d, cs.at[ph, d - 2, pl.ds(0, rows)], cr.at[ph, slot - 2, pl.ds(0, rows)],
                c_send.at[ph, d - 2], c_recv.at[ph, slot - 2],
            )
        return make

    def solved_copy(ph):
        def make(d, slot):
            if d < 4:
                return remote(
                    d, outs.at[ph, d - 2], outr.at[ph, slot - 2],
                    a_send.at[ph, d - 2], a_recv.at[ph, slot - 2],
                )
            return remote(
                d, outs.at[ph, d - 8], c2r.at[ph, slot - 8],
                c2_send.at[ph, d - 8], c2_recv.at[ph, slot - 8],
            )
        return make

    def one_round(outer, k):
        first = isinstance(k, int)
        ph = outer * ROUNDS + k
        om = relax_weight(0)
        if not first:
            for i in range(1, ROUNDS):
                om = jnp.where(k == i, jnp.float32(relax_weight(i)), om)
        for at in range(0, ROWS * 8, PIECE):
            here = pl.ds(at, PIECE)
            if first:
                e1[pl.ds(at + 8, PIECE)] = om * reduce_x(tgt[here], xfac(here))
            else:
                v, u = update(tgt, e0, at)
                e1[pl.ds(at + 8, PIECE)] = v + om * reduce_x(u, xfac(here))
        for s in range(2):
            near, far = (0, 1) if s == 0 else (7, 6)
            cs[ph, s, pl.ds(0, ROWS)] = e1[col(near, ROWS, 1)]
            cs[ph, s, pl.ds(ROWS, ROWS)] = e1[col(far, ROWS, 1)]
            if first:
                cs[ph, s, pl.ds(2 * ROWS, ROWS)] = tgt[col(near)]
        make = col_copy(ph, (3 if first else 2) * ROWS)
        exchange_start((2, 3), make)
        if first and outer == 0:
            rest_of_setup()
        if not first:
            exchange_wait((2, 3, 8, 9), solved_copy(ph))
            for z in range(ROWS):
                at, here = pl.ds((z + 1) * 8, 8), pl.ds(z * 8, 8)
                left = jnp.broadcast_to(outr[ph, 0, pl.ds(z, 1)], (8, LANES))
                right = jnp.broadcast_to(outr[ph, 1, pl.ds(z, 1)], (8, LANES))
                e1[at] = e1[at] + om * (gx[0, here] * left + gx[1, here] * right)
        for at in range(0, ROWS * 8, PIECE):
            here = pl.ds(at, PIECE)
            v, u = update(tgt, e1, at)
            e2[pl.ds(at + 8, PIECE)] = v + om * reduce_y(u, [yf[i, here] for i in range(7)])
        exchange_wait((2, 3), make)
        for s in range(2):
            near, far = cr[ph, s, pl.ds(0, ROWS)], cr[ph, s, pl.ds(ROWS, ROWS)]
            if first:
                tside[s] = cr[ph, s, pl.ds(2 * ROWS, ROWS)]
            else:
                beyond, inner = c2r[ph, s], e0[col(7 * s, ROWS, 1)]
                left, right = (beyond, inner) if s == 0 else (inner, beyond)
                g = [gr[s, pl.ds(i * ROWS, ROWS)] for i in range(4)]
                near = near + om * (g[0] * left + g[2] * right)
                far = far + om * (g[1] * left + g[3] * right)
            u = tside[s] - near
            u = u + sco[s, 0] * roll_z(near, 1) + sco[s, 1] * roll_z(near, -1)
            u = u + sco[s, 2] * far + sco[s, 3] * e1[col(7 * s, ROWS, 1)]
            u = u + sco[s, 4] * roll_y(near, 1) + sco[s, 5] * roll_y(near, -1)
            beside = near + om * reduce_y(u, [syf[s, i] for i in range(7)])
            ub[col(7 * s)] = cx[s] * beside
            at = col(7 * s, ROWS, 1)
            e2[at] = e2[at] + om * reduce_y(cx[s] * near, [ycf[s, i] for i in range(7)])
        for at in range(0, ROWS * 8, PIECE):
            v, u = update(tgt, e2, at)
            u = (u + ub[pl.ds(at, PIECE)]).reshape(PIECE // CH, BL, 8, LANES)
            m, iv, up = (zf[i, pl.ds(at, PIECE)].reshape(u.shape) for i in range(3))
            v = v.reshape(u.shape)
            fw = [u[:, 0]]
            for i in range(1, BL):
                fw.append(u[:, i] - m[:, i] * fw[-1])
            nxt = None
            for i in range(BL - 1, -1, -1):
                x = fw[i] * iv[:, i]
                nxt = x if nxt is None else x - up[:, i] * nxt
                new = v[:, i] + om * nxt
                for c in range(PIECE // CH):
                    e0[pl.ds(at + c * CH + (i + 1) * 8, 8)] = new[c]

        def send_next():
            for s in range(2):
                outs[ph + 1, s] = e0[col(7 * s, ROWS, 1)]
            exchange_start((2, 3, 8, 9), solved_copy(ph + 1))

        if first:
            send_next()
        else:
            pl.when(k < ROUNDS - 1)(send_next)

    def mid_copy(d, slot):
        if d < 2:
            a, b = corr.at[pl.ds(0 if d == 0 else 120, 72)], mzr.at[slot]
        elif d < 4:
            a, b = mx.at[d - 2], mxr.at[slot - 2]
        else:
            z, s = divmod(d - 4, 2)
            a, b = mx.at[s, pl.ds(16 * z, 8)], mdr.at[slot - 4]
        return remote(d, a, b, m_send.at[d], m_recv.at[slot])

    def end_copy(d, slot):
        a = corr.at[pl.ds(0 if d == 0 else 160, 32)]
        return remote(d, a, fzr.at[slot], f_send.at[d], f_recv.at[slot])

    for outer in range(OUTER):
        for s in range(2):
            ub[col(7 * s)] = cx[s] * spre[s]
        for c in range(0, CHUNKS, PIECE // CH):
            rows = [active(rows_of(i)) for i in range(c, c + PIECE // CH)]
            here = pl.ds(c * CH, PIECE)
            tgt[here] = update(isrc, pres, c * CH, jnp.concatenate(rows))[1] + ub[here]
        one_round(outer, 0)
        if outer == 0:
            exchange_wait((2, 3), answer_copy)

        def step(k, carry, outer=outer):
            one_round(outer, k)
            return carry

        lax.fori_loop(1, ROUNDS, step, 0)
        for c in range(CHUNKS):
            rows = rows_of(c)
            band = (rows < OV + low) | (rows >= OV + OWN - high)
            w = active(rows) * jnp.where(band, 0.5, 1.0)
            corr[pl.ds(c * CH, CH)] = w * e0[pl.ds((c * 8 + 1) * 8, CH)]
        if outer == 0:
            for s in range(2):
                mx[s] = corr[col(7 * s)]
            exchange_start(range(8), mid_copy)
            pres[pl.ds(8, ROWS * 8)] = pres[pl.ds(8, ROWS * 8)] + corr[...]
            exchange_wait(range(8), mid_copy)
            for z in range(2):
                at = pl.ds(0 if z == 0 else 17 * 8, 72)
                pres[at] = pres[at] + mzr[z]
            for s in range(2):
                spre[s] = spre[s] + mxr[s]
                for z in range(2):
                    at = pl.ds(16 * z, 8)
                    spre[s, at] = spre[s, at] + mdr[2 * z + s]
        else:
            exchange_start((0, 1), end_copy)
            pres[pl.ds(8, ROWS * 8)] = pres[pl.ds(8, ROWS * 8)] + corr[...]
            exchange_wait((0, 1), end_copy)
            for z in range(2):
                at = pl.ds(40 if z == 0 else 17 * 8, 32)
                pres[at] = pres[at] + fzr[z]
    out[...] = pres[pl.ds(40, OWN * 8)].reshape(OWN, 8, LANES)


def on_device(facies, facies_perm, perm_scale, source, pressure_start, intersection_depth):
    assert source.shape == (OWN, 8, LANES)
    f32 = jnp.float32

    def buf(*shape):
        return pltpu.VMEM(shape, f32)

    field, wide = (ROWS * 8, LANES), (WIDE * 8, LANES)
    phases, own, dma = OUTER * ROUNDS, source.shape, pltpu.SemaphoreType.DMA
    scratch = [
        pltpu.VMEM(own, jnp.int32), buf(*own), buf(*own), buf(*own),
        pltpu.SMEM(facies_perm.shape, f32), pltpu.SMEM(intersection_depth.shape, jnp.int32),
        dma((6,)), buf(2, 4 * ROWS, LANES), buf(2, 4 * ROWS, LANES),
        *[buf(phases, 2, ROWS, LANES)] * 3, buf(2, 7, ROWS, LANES),
        buf(2, 112, LANES), buf(2, 48, LANES), buf(4, 24, LANES),
        buf(2, 112, LANES), buf(2, 48, LANES), buf(4, 24, LANES),
        buf(2, ROWS, LANES), buf(2, 72, LANES), buf(2, ROWS, LANES), buf(4, 8, LANES),
        buf(2, 32, LANES), buf(phases, 2, 3 * ROWS, LANES), buf(phases, 2, 3 * ROWS, LANES),
        buf(*wide), buf(*wide), buf(2, 2, 32, LANES), buf(2, ROWS, LANES),
        buf(*field), buf(*field), buf(2, ROWS, LANES),
        buf(*wide), buf(*wide), buf(*wide), buf(*field), buf(*field),
        buf(6, *field), buf(4, *field), buf(7, *field), buf(3, *field),
        buf(2, *field), buf(2, ROWS, LANES), buf(2, 6, ROWS, LANES), buf(2, 7, ROWS, LANES),
    ]
    sems = [dma((n,)) for n in (8, 8, 8, 8, 2, 2, 2, 2)]
    sems += [dma((phases, 2)) for _ in range(6)]
    return pl.pallas_call(
        kernel,
        out_shape=jax.ShapeDtypeStruct(source.shape, f32),
        in_specs=[pl.BlockSpec(memory_space=pltpu.HBM)] * 6,
        out_specs=pl.BlockSpec(memory_space=pltpu.VMEM),
        scratch_shapes=scratch + sems,
        compiler_params=pltpu.CompilerParams(
            collective_id=0, has_side_effects=True, vmem_limit_bytes=60 * 1024 * 1024
        ),
        name="schwarz",
    )(facies, facies_perm, perm_scale, source, pressure_start, intersection_depth)


def solution(mesh):
    return jax.shard_map(
        on_device,
        mesh=mesh,
        in_specs=(
            P("sub", "grp", None),
            P(),
            P("sub", "grp", None),
            P("sub", "grp", None),
            P("sub", "grp", None),
            P(),
        ),
        out_specs=P("sub", "grp", None),
        check_vma=False,
    )
```

```python
import functools
import math

import jax
import jax.numpy as jnp
from jax import lax
from jax.experimental import pallas as pl
from jax.experimental.pallas import tpu as pltpu
from jax.sharding import PartitionSpec as P

OV = 4
BL = 8
ROUNDS = 4
OUTER = 2
FACIES = 8
STORE = 0.02
MESH = pl.DeviceIdType.MESH

OWN = 16
ROWS = OWN + 2 * OV
WIDE = ROWS + 2
LANES = 128
CHUNKS = ROWS // BL
CH = BL * 8
PIECE = CH

DIRS = (
    (-1, 0), (1, 0), (0, -1), (0, 1), (-1, -1), (-1, 1), (1, -1), (1, 1), (0, -2), (0, 2)
)
OPP = tuple(DIRS.index((-a, -b)) for a, b in DIRS)


def relax_weight(k):
    return 1.0 / (1.4 + 0.6 * math.cos(math.pi * (2 * k + 1) / (2 * ROUNDS)))


def harmonic(a, b):
    return 2.0 * a * b / jnp.maximum(a + b, 1e-30)


def roll_x(v, s):
    return pltpu.roll(v.reshape(v.shape[0] // 8, 8, LANES), s % 8, 1).reshape(v.shape)


def roll_y(v, s):
    return pltpu.roll(v, s % LANES, 1)


def roll_z(v, s):
    return pltpu.roll(v, s % v.shape[0], 0)


def reduce_factors(low, high, roll):
    l, u, d = -low, -high, None
    parts = []
    for s in (1, 2, 4):
        if d is None:
            a, b, d = low, high, jnp.ones_like(low)
        else:
            rd = 1.0 / d
            a, b = -l * roll(rd, s), -u * roll(rd, -s)
        d = d + a * roll(u, s) + b * roll(l, -s)
        l, u = a * roll(l, s), b * roll(u, -s)
        parts += [a, b]
    return parts + [1.0 / d]


def reduce_x(r, f):
    a1, b1, a2, b2, c3, iv = f
    r = r + a1 * roll_x(r, 1) + b1 * roll_x(r, -1)
    r = r + a2 * roll_x(r, 2) + b2 * roll_x(r, -2)
    r = r + c3 * roll_x(r, 4)
    return r * iv


def reduce_y(r, f):
    a1, b1, a2, b2, a3, b3, iv = f
    r = r + a1 * roll_y(r, 1) + b1 * roll_y(r, -1)
    r = r + a2 * roll_y(r, 2) + b2 * roll_y(r, -2)
    r = r + a3 * roll_y(r, 4) + b3 * roll_y(r, -4)
    return r * iv


def col(x, planes=ROWS, first=0):
    return pl.ds(first * 8 + x, planes, stride=8)


def kernel(
    fac_h, fperm_h, pscale_h, src_h, p0_h, depth_h, out,
    fac, pscale, src, p0, fperm, depth, in_sem, gs, gr, c2r, outs, outr, ycf,
    zs, xs, ds, zr, xr, dr, mx, mzr, mxr, mdr, fzr, cs, cr,
    perm, pres, sper, spre, isrc, tgt, tside, e0, e1, e2, ub, corr,
    co, xf, yf, zf, gx, cx, sco, syf,
    i_send, i_recv, m_send, m_recv, f_send, f_recv, g_send, g_recv,
    c_send, c_recv, c2_send, c2_recv, a_send, a_recv,
):
    n_sub, n_grp = lax.axis_size("sub"), lax.axis_size("grp")
    sub, grp = lax.axis_index("sub"), lax.axis_index("grp")
    has_axis = {
        (-1, 0): sub > 0,
        (1, 0): sub < n_sub - 1,
        (0, -1): grp > 0,
        (0, 1): grp < n_grp - 1,
        (0, -2): grp > 1,
        (0, 2): grp < n_grp - 2,
    }
    has = []
    for dz, dx in DIRS:
        if dz and dx:
            has.append(jnp.logical_and(has_axis[(dz, 0)], has_axis[(0, dx)]))
        else:
            has.append(has_axis[(dz, dx)])

    def peer(d):
        return {"sub": sub + DIRS[d][0], "grp": grp + DIRS[d][1]}

    def remote(d, a, b, s_sem, r_sem):
        return pltpu.make_async_remote_copy(
            src_ref=a, dst_ref=b, send_sem=s_sem, recv_sem=r_sem,
            device_id=peer(d), device_id_type=MESH,
        )

    def exchange_start(dirs, make):
        for d in dirs:
            @pl.when(has[d])
            def _(d=d):
                make(d, OPP[d]).start()

    def exchange_wait(dirs, make):
        for d in dirs:
            @pl.when(has[d])
            def _(d=d):
                make(d, d).wait_recv()

    def exchange_sent(dirs, makes):
        for d in dirs:
            @pl.when(has[d])
            def _(d=d):
                for make in makes:
                    make(d, OPP[d]).wait_send()

    barrier = pltpu.get_barrier_semaphore()
    for d in range(len(DIRS)):
        @pl.when(has[d])
        def _(d=d):
            pl.semaphore_signal(barrier, inc=1, device_id=peer(d), device_id_type=MESH)

    loads = [
        pltpu.make_async_copy(a, b, in_sem.at[i])
        for i, (a, b) in enumerate((
            (fac_h, fac), (pscale_h, pscale), (p0_h, p0), (src_h, src),
            (fperm_h, fperm), (depth_h, depth),
        ))
    ]
    for load in loads:
        load.start()

    for d in range(len(DIRS)):
        @pl.when(jnp.logical_not(has[d]))
        def _(d=d):
            if d < 2:
                zr[d] = jnp.zeros(zr.shape[1:], jnp.float32)
                mzr[d] = jnp.zeros(mzr.shape[1:], jnp.float32)
                fzr[d] = jnp.zeros(fzr.shape[1:], jnp.float32)
            elif d < 4:
                xr[d - 2] = jnp.zeros(xr.shape[1:], jnp.float32)
                mxr[d - 2] = jnp.zeros(mxr.shape[1:], jnp.float32)
                gr[d - 2] = jnp.zeros(gr.shape[1:], jnp.float32)
                for ph in range(cr.shape[0]):
                    cr[ph, d - 2] = jnp.zeros(cr.shape[2:], jnp.float32)
                    outr[ph, d - 2] = jnp.zeros(outr.shape[2:], jnp.float32)
            elif d < 8:
                dr[d - 4] = jnp.zeros(dr.shape[1:], jnp.float32)
                mdr[d - 4] = jnp.zeros(mdr.shape[1:], jnp.float32)
            else:
                for ph in range(c2r.shape[0]):
                    c2r[ph, d - 8] = jnp.zeros(c2r.shape[2:], jnp.float32)

    for i in (0, 1, 4):
        loads[i].wait()
    kinds = fac[...]
    own = jnp.zeros(kinds.shape, jnp.float32)
    for kind in range(FACIES):
        own = jnp.where(kinds == kind, fperm[kind], own)
    perm[pl.ds(40, OWN * 8)] = (own * pscale[...]).reshape(OWN * 8, LANES)
    for s in range(2):
        near, far = (0, 1) if s == 0 else (7, 6)
        zs[s, pl.ds(0, 40)] = perm[pl.ds(40 if s == 0 else 128, 40)]
        xs[s, pl.ds(0, 16)] = perm[col(near, 16, 5)]
        xs[s, pl.ds(16, 16)] = perm[col(far, 16, 5)]
        for z in range(2):
            at_rows = 5 if z == 0 else 13
            ds[2 * z + s, pl.ds(0, 8)] = perm[col(near, 8, at_rows)]
            ds[2 * z + s, pl.ds(8, 8)] = perm[col(far, 8, at_rows)]

    def init_copy(part):
        def make(d, slot):
            if d < 2:
                at, a, b = (pl.ds(0, 40), pl.ds(40, 72))[part], zs.at[d], zr.at[slot]
            elif d < 4:
                at, a, b = (pl.ds(0, 32), pl.ds(32, 16))[part], xs.at[d - 2], xr.at[slot - 2]
            else:
                at, a, b = (pl.ds(0, 16), pl.ds(16, 8))[part], ds.at[d - 4], dr.at[slot - 4]
            return remote(d, a.at[at], b.at[at], i_send.at[part, d], i_recv.at[part, slot])
        return make

    pl.semaphore_wait(barrier, sum(jnp.where(h, 1, 0) for h in has))
    exchange_start(range(8), init_copy(0))
    for i in (2, 3, 5):
        loads[i].wait()
    pres[pl.ds(40, OWN * 8)] = p0[...].reshape(OWN * 8, LANES)
    isrc[pl.ds(32, OWN * 8)] = src[...].reshape(OWN * 8, LANES)
    for s in range(2):
        near = 7 * s
        zs[s, pl.ds(40, 40)] = pres[pl.ds(40 if s == 0 else 128, 40)]
        zs[s, pl.ds(80, 32)] = isrc[pl.ds(32 if s == 0 else 128, 32)]
        xs[s, pl.ds(32, 16)] = pres[col(near, 16, 5)]
        for z in range(2):
            ds[2 * z + s, pl.ds(16, 8)] = pres[col(near, 8, 5 if z == 0 else 13)]
    exchange_start(range(8), init_copy(1))

    low = jnp.where(sub > 0, depth[jnp.maximum(sub - 1, 0)], 0)
    high = jnp.where(sub < n_sub - 1, depth[jnp.minimum(sub, n_sub - 2)], 0)

    def active(rows):
        inside = (rows >= OV - low) & (rows < OV + OWN + high)
        return jnp.where(inside, 1.0, 0.0)

    def rows_of(c):
        return lax.broadcasted_iota(jnp.int32, (8, 8, LANES), 0).reshape(CH, LANES) + 8 * c

    lane = lax.broadcasted_iota(jnp.int32, (CH, LANES), 1)
    lane2 = lax.broadcasted_iota(jnp.int32, (ROWS, LANES), 1)
    row2 = lax.broadcasted_iota(jnp.int32, (ROWS, LANES), 0)
    subl = lax.broadcasted_iota(jnp.int32, (8, 8, LANES), 1).reshape(CH, LANES)
    zeros_plane = jnp.zeros((8, LANES), jnp.float32)
    for e in (e0, e1, e2):
        e[pl.ds(0, 8)] = zeros_plane
        e[pl.ds((ROWS + 1) * 8, 8)] = zeros_plane

    exchange_wait(range(8), init_copy(0))
    perm[pl.ds(0, 40)] = zr[0, pl.ds(0, 40)]
    perm[pl.ds(168, 40)] = zr[1, pl.ds(0, 40)]
    for s in range(2):
        for f in range(2):
            sper[s, f, pl.ds(5, 16)] = xr[s, pl.ds(16 * f, 16)]
            sper[s, f, pl.ds(0, 5)] = dr[s, pl.ds(8 * f + 3, 5)]
            sper[s, f, pl.ds(21, 5)] = dr[2 + s, pl.ds(8 * f, 5)]
        ub[col(7 * s)] = sper[s, 0, pl.ds(1, ROWS)]

    for c in range(CHUNKS):
        here = pl.ds(c * CH, CH)
        mid = perm[pl.ds((c * 8 + 1) * 8, CH)]
        edge = ub[here]
        fb = harmonic(perm[pl.ds(c * CH, CH)], mid)
        fa = harmonic(mid, perm[pl.ds((c * 8 + 2) * 8, CH)])
        fl = harmonic(jnp.where(subl == 0, edge, roll_x(mid, 1)), mid)
        fr = harmonic(mid, jnp.where(subl == 7, edge, roll_x(mid, -1)))
        ff = harmonic(jnp.where(lane == 0, 0.0, roll_y(mid, 1)), mid)
        fk = harmonic(mid, jnp.where(lane == LANES - 1, 0.0, roll_y(mid, -1)))
        act = active(rows_of(c))
        inv = act / (STORE + fb + fa + fl + fr + ff + fk)
        fl, fr = fl * inv, fr * inv
        ub[here] = jnp.where(subl == 0, fl, fr)
        fl, fr = jnp.where(subl == 0, 0.0, fl), jnp.where(subl == 7, 0.0, fr)
        fb, fa, ff, fk = fb * inv, fa * inv, ff * inv, fk * inv
        for i, f in enumerate((fb, fa, fl, fr, ff, fk)):
            co[i, here] = f
        zf[0, here] = inv
        a1, b1, a2, b2, a3, b3, iv = reduce_factors(fl, fr, roll_x)
        for i, f in enumerate((a2, b2, a3 + b3, iv)):
            xf[i, here] = f
    for s in range(2):
        cx[s] = ub[col(7 * s)]

    def xfac(here):
        return [co[2, here], co[3, here]] + [xf[i, here] for i in range(4)]

    exchange_wait(range(8), init_copy(1))
    pres[pl.ds(0, 40)] = zr[0, pl.ds(40, 40)]
    isrc[pl.ds(0, 32)] = zr[0, pl.ds(80, 32)]
    pres[pl.ds(168, 40)] = zr[1, pl.ds(40, 40)]
    isrc[pl.ds(160, 32)] = zr[1, pl.ds(80, 32)]
    isrc[...] = isrc[...] * zf[0]
    for s in range(2):
        spre[s, pl.ds(4, 16)] = xr[s, pl.ds(32, 16)]
        spre[s, pl.ds(0, 4)] = dr[s, pl.ds(20, 4)]
        spre[s, pl.ds(20, 4)] = dr[2 + s, pl.ds(16, 4)]
    for c in range(CHUNKS):
        gx[0, pl.ds(c * CH, CH)] = ub[pl.ds(c * CH, CH)]
        ub[pl.ds(c * CH, CH)] = jnp.zeros((CH, LANES), jnp.float32)

    def answer_copy(d, slot):
        return remote(
            d, gs.at[d - 2], gr.at[slot - 2], g_send.at[d - 2], g_recv.at[slot - 2]
        )

    def rest_of_setup():
        for c in range(CHUNKS):
            here = pl.ds(c * CH, CH)
            fb, fa, ff, fk = (co[i, here] for i in (0, 1, 4, 5))
            fy = reduce_factors(
                jnp.where(lane % BL == 0, 0.0, ff), jnp.where(lane % BL == BL - 1, 0.0, fk), roll_y
            )
            for i, f in enumerate(fy):
                yf[i, here] = f
            lz = -fb * active(rows_of(c) - 1)
            uz = -fa * active(rows_of(c) + 1)
            d = None
            for i in range(BL):
                at = pl.ds(c * CH + i * 8, 8)
                part = slice(i * 8, i * 8 + 8)
                if i == 0:
                    m, d = zeros_plane, jnp.ones((8, LANES), jnp.float32)
                else:
                    m = lz[part] / d
                    d = 1.0 - m * uz[(i - 1) * 8 : i * 8]
                zf[0, at] = m
                zf[1, at] = 1.0 / d
                zf[2, at] = uz[part] / d
        for c in range(CHUNKS):
            here = pl.ds(c * CH, CH)
            edge, f = gx[0, here], xfac(here)
            for s in range(2):
                gx[s, here] = reduce_x(jnp.where(subl == 7 * s, edge, 0.0), f)
        for s in range(2):
            near, far = (0, 1) if s == 0 else (7, 6)
            for i in range(2):
                gs[s, pl.ds(2 * i * ROWS, ROWS)] = gx[i, col(near)]
                gs[s, pl.ds((2 * i + 1) * ROWS, ROWS)] = gx[i, col(far)]

        exchange_start((2, 3), answer_copy)

        for s in range(2):
            for i in range(7):
                ycf[s, i] = yf[i, col(7 * s)]

        for s in range(2):
            mid = sper[s, 0, pl.ds(1, ROWS)]
            fb = harmonic(sper[s, 0, pl.ds(0, ROWS)], mid)
            fa = harmonic(mid, sper[s, 0, pl.ds(2, ROWS)])
            fx = harmonic(mid, sper[s, 1, pl.ds(1, ROWS)])
            fo = harmonic(mid, perm[col(7 * s, ROWS, 1)])
            ff = harmonic(jnp.where(lane2 == 0, 0.0, roll_y(mid, 1)), mid)
            fk = harmonic(mid, jnp.where(lane2 == LANES - 1, 0.0, roll_y(mid, -1)))
            inv = active(row2) / (STORE + fb + fa + fx + fo + ff + fk)
            fb = jnp.where(row2 == 0, 0.0, fb * inv)
            fa = jnp.where(row2 == ROWS - 1, 0.0, fa * inv)
            ff, fk = ff * inv, fk * inv
            for i, f in enumerate((fb, fa, fx * inv, fo * inv, ff, fk)):
                sco[s, i] = f
            fy = reduce_factors(
                jnp.where(lane2 % BL == 0, 0.0, ff), jnp.where(lane2 % BL == BL - 1, 0.0, fk), roll_y
            )
            for i, f in enumerate(fy):
                syf[s, i] = f

    def update(t, e, at, scale=None):
        here = pl.ds(at, PIECE)
        v = e[pl.ds(at + 8, PIECE)]
        u = t[here] - (v if scale is None else v * scale)
        u = u + co[0, here] * e[here] + co[1, here] * e[pl.ds(at + 16, PIECE)]
        u = u + co[2, here] * roll_x(v, 1) + co[3, here] * roll_x(v, -1)
        return v, u + co[4, here] * roll_y(v, 1) + co[5, here] * roll_y(v, -1)

    def col_copy(ph, rows):
        def make(d, slot):
            return remote(
                d, cs.at[ph, d - 2, pl.ds(0, rows)], cr.at[ph, slot - 2, pl.ds(0, rows)],
                c_send.at[ph, d - 2], c_recv.at[ph, slot - 2],
            )
        return make

    def solved_copy(ph):
        def make(d, slot):
            if d < 4:
                return remote(
                    d, outs.at[ph, d - 2], outr.at[ph, slot - 2],
                    a_send.at[ph, d - 2], a_recv.at[ph, slot - 2],
                )
            return remote(
                d, outs.at[ph, d - 8], c2r.at[ph, slot - 8],
                c2_send.at[ph, d - 8], c2_recv.at[ph, slot - 8],
            )
        return make

    def one_round(outer, k):
        first = isinstance(k, int)
        ph = outer * ROUNDS + k
        om = relax_weight(0)
        if not first:
            for i in range(1, ROUNDS):
                om = jnp.where(k == i, jnp.float32(relax_weight(i)), om)
        for at in range(0, ROWS * 8, PIECE):
            here = pl.ds(at, PIECE)
            if first:
                e1[pl.ds(at + 8, PIECE)] = om * reduce_x(tgt[here], xfac(here))
            else:
                v, u = update(tgt, e0, at)
                e1[pl.ds(at + 8, PIECE)] = v + om * reduce_x(u, xfac(here))
        for s in range(2):
            near, far = (0, 1) if s == 0 else (7, 6)
            cs[ph, s, pl.ds(0, ROWS)] = e1[col(near, ROWS, 1)]
            cs[ph, s, pl.ds(ROWS, ROWS)] = e1[col(far, ROWS, 1)]
            if first:
                cs[ph, s, pl.ds(2 * ROWS, ROWS)] = tgt[col(near)]
        make = col_copy(ph, (3 if first else 2) * ROWS)
        exchange_start((2, 3), make)
        if first and outer == 0:
            rest_of_setup()
        if not first:
            exchange_wait((2, 3, 8, 9), solved_copy(ph))
            for z in range(ROWS):
                at, here = pl.ds((z + 1) * 8, 8), pl.ds(z * 8, 8)
                left = jnp.broadcast_to(outr[ph, 0, pl.ds(z, 1)], (8, LANES))
                right = jnp.broadcast_to(outr[ph, 1, pl.ds(z, 1)], (8, LANES))
                e1[at] = e1[at] + om * (gx[0, here] * left + gx[1, here] * right)
        for at in range(0, ROWS * 8, PIECE):
            here = pl.ds(at, PIECE)
            v, u = update(tgt, e1, at)
            e2[pl.ds(at + 8, PIECE)] = v + om * reduce_y(u, [yf[i, here] for i in range(7)])
        exchange_wait((2, 3), make)
        for s in range(2):
            near, far = cr[ph, s, pl.ds(0, ROWS)], cr[ph, s, pl.ds(ROWS, ROWS)]
            if first:
                tside[s] = cr[ph, s, pl.ds(2 * ROWS, ROWS)]
            else:
                beyond, inner = c2r[ph, s], e0[col(7 * s, ROWS, 1)]
                left, right = (beyond, inner) if s == 0 else (inner, beyond)
                g = [gr[s, pl.ds(i * ROWS, ROWS)] for i in range(4)]
                near = near + om * (g[0] * left + g[2] * right)
                far = far + om * (g[1] * left + g[3] * right)
            u = tside[s] - near
            u = u + sco[s, 0] * roll_z(near, 1) + sco[s, 1] * roll_z(near, -1)
            u = u + sco[s, 2] * far + sco[s, 3] * e1[col(7 * s, ROWS, 1)]
            u = u + sco[s, 4] * roll_y(near, 1) + sco[s, 5] * roll_y(near, -1)
            beside = near + om * reduce_y(u, [syf[s, i] for i in range(7)])
            ub[col(7 * s)] = cx[s] * beside
            at = col(7 * s, ROWS, 1)
            e2[at] = e2[at] + om * reduce_y(cx[s] * near, [ycf[s, i] for i in range(7)])
        for at in range(0, ROWS * 8, PIECE):
            v, u = update(tgt, e2, at)
            u = (u + ub[pl.ds(at, PIECE)]).reshape(PIECE // CH, BL, 8, LANES)
            m, iv, up = (zf[i, pl.ds(at, PIECE)].reshape(u.shape) for i in range(3))
            v = v.reshape(u.shape)
            fw = [u[:, 0]]
            for i in range(1, BL):
                fw.append(u[:, i] - m[:, i] * fw[-1])
            nxt = None
            for i in range(BL - 1, -1, -1):
                x = fw[i] * iv[:, i]
                nxt = x if nxt is None else x - up[:, i] * nxt
                new = v[:, i] + om * nxt
                for c in range(PIECE // CH):
                    e0[pl.ds(at + c * CH + (i + 1) * 8, 8)] = new[c]

        def send_next():
            for s in range(2):
                outs[ph + 1, s] = e0[col(7 * s, ROWS, 1)]
            exchange_start((2, 3, 8, 9), solved_copy(ph + 1))

        if first:
            send_next()
        else:
            pl.when(k < ROUNDS - 1)(send_next)

    def mid_copy(d, slot):
        if d < 2:
            a, b = corr.at[pl.ds(0 if d == 0 else 120, 72)], mzr.at[slot]
        elif d < 4:
            a, b = mx.at[d - 2], mxr.at[slot - 2]
        else:
            z, s = divmod(d - 4, 2)
            a, b = mx.at[s, pl.ds(16 * z, 8)], mdr.at[slot - 4]
        return remote(d, a, b, m_send.at[d], m_recv.at[slot])

    def end_copy(d, slot):
        a = corr.at[pl.ds(0 if d == 0 else 160, 32)]
        return remote(d, a, fzr.at[slot], f_send.at[d], f_recv.at[slot])

    for outer in range(OUTER):
        for s in range(2):
            ub[col(7 * s)] = cx[s] * spre[s]
        for c in range(0, CHUNKS, PIECE // CH):
            rows = [active(rows_of(i)) for i in range(c, c + PIECE // CH)]
            here = pl.ds(c * CH, PIECE)
            tgt[here] = update(isrc, pres, c * CH, jnp.concatenate(rows))[1] + ub[here]
        one_round(outer, 0)
        if outer == 0:
            exchange_wait((2, 3), answer_copy)

        def step(k, carry, outer=outer):
            one_round(outer, k)
            return carry

        lax.fori_loop(1, ROUNDS, step, 0)
        if outer == 1:
            exchange_sent(range(8), [mid_copy])
        for c in range(CHUNKS):
            rows = rows_of(c)
            band = (rows < OV + low) | (rows >= OV + OWN - high)
            w = active(rows) * jnp.where(band, 0.5, 1.0)
            corr[pl.ds(c * CH, CH)] = w * e0[pl.ds((c * 8 + 1) * 8, CH)]
        if outer == 0:
            for s in range(2):
                mx[s] = corr[col(7 * s)]
            exchange_start(range(8), mid_copy)
            pres[pl.ds(8, ROWS * 8)] = pres[pl.ds(8, ROWS * 8)] + corr[...]
            exchange_wait(range(8), mid_copy)
            for z in range(2):
                at = pl.ds(0 if z == 0 else 17 * 8, 72)
                pres[at] = pres[at] + mzr[z]
            for s in range(2):
                spre[s] = spre[s] + mxr[s]
                for z in range(2):
                    at = pl.ds(16 * z, 8)
                    spre[s, at] = spre[s, at] + mdr[2 * z + s]
        else:
            exchange_start((0, 1), end_copy)
            later = [k for k in range(OUTER * ROUNDS) if k % ROUNDS]
            exchange_sent(range(8), [init_copy(0), init_copy(1)])
            makes = [col_copy(k, (2 if k % ROUNDS else 3) * ROWS) for k in range(OUTER * ROUNDS)]
            makes += [solved_copy(k) for k in later]
            exchange_sent((2, 3), makes + [answer_copy])
            exchange_sent((8, 9), [solved_copy(k) for k in later])
            exchange_sent((0, 1), [end_copy])
            pres[pl.ds(8, ROWS * 8)] = pres[pl.ds(8, ROWS * 8)] + corr[...]
            exchange_wait((0, 1), end_copy)
            for z in range(2):
                at = pl.ds(40 if z == 0 else 17 * 8, 32)
                pres[at] = pres[at] + fzr[z]
    out[...] = pres[pl.ds(40, OWN * 8)].reshape(OWN, 8, LANES)


def on_device(facies, facies_perm, perm_scale, source, pressure_start, intersection_depth):
    assert source.shape == (OWN, 8, LANES)
    f32 = jnp.float32

    def buf(*shape):
        return pltpu.VMEM(shape, f32)

    field, wide = (ROWS * 8, LANES), (WIDE * 8, LANES)
    phases, own, dma = OUTER * ROUNDS, source.shape, pltpu.SemaphoreType.DMA
    scratch = [
        pltpu.VMEM(own, jnp.int32), buf(*own), buf(*own), buf(*own),
        pltpu.SMEM(facies_perm.shape, f32), pltpu.SMEM(intersection_depth.shape, jnp.int32),
        dma((6,)), buf(2, 4 * ROWS, LANES), buf(2, 4 * ROWS, LANES),
        *[buf(phases, 2, ROWS, LANES)] * 3, buf(2, 7, ROWS, LANES),
        buf(2, 112, LANES), buf(2, 48, LANES), buf(4, 24, LANES),
        buf(2, 112, LANES), buf(2, 48, LANES), buf(4, 24, LANES),
        buf(2, ROWS, LANES), buf(2, 72, LANES), buf(2, ROWS, LANES), buf(4, 8, LANES),
        buf(2, 32, LANES), buf(phases, 2, 3 * ROWS, LANES), buf(phases, 2, 3 * ROWS, LANES),
        buf(*wide), buf(*wide), buf(2, 2, 32, LANES), buf(2, ROWS, LANES),
        buf(*field), buf(*field), buf(2, ROWS, LANES),
        buf(*wide), buf(*wide), buf(*wide), buf(*field), buf(*field),
        buf(6, *field), buf(4, *field), buf(7, *field), buf(3, *field),
        buf(2, *field), buf(2, ROWS, LANES), buf(2, 6, ROWS, LANES), buf(2, 7, ROWS, LANES),
    ]
    sems = [dma((2, 8)), dma((2, 8))] + [dma((n,)) for n in (8, 8, 2, 2, 2, 2)]
    sems += [dma((phases, 2)) for _ in range(6)]
    return pl.pallas_call(
        kernel,
        out_shape=jax.ShapeDtypeStruct(source.shape, f32),
        in_specs=[pl.BlockSpec(memory_space=pltpu.HBM)] * 6,
        out_specs=pl.BlockSpec(memory_space=pltpu.VMEM),
        scratch_shapes=scratch + sems,
        compiler_params=pltpu.CompilerParams(
            collective_id=0, has_side_effects=True, vmem_limit_bytes=60 * 1024 * 1024
        ),
        name="schwarz",
    )(facies, facies_perm, perm_scale, source, pressure_start, intersection_depth)


def solution(mesh):
    return jax.shard_map(
        on_device,
        mesh=mesh,
        in_specs=(
            P("sub", "grp", None),
            P(),
            P("sub", "grp", None),
            P("sub", "grp", None),
            P("sub", "grp", None),
            P(),
        ),
        out_specs=P("sub", "grp", None),
        check_vma=False,
    )
```

```python
import functools
import math

import jax
import jax.numpy as jnp
from jax import lax
from jax.experimental import pallas as pl
from jax.experimental.pallas import tpu as pltpu
from jax.sharding import PartitionSpec as P

OV = 4
BL = 8
ROUNDS = 4
OUTER = 2
FACIES = 8
STORE = 0.02
MESH = pl.DeviceIdType.MESH

OWN = 16
ROWS = OWN + 2 * OV
WIDE = ROWS + 2
LANES = 128
CHUNKS = ROWS // BL
CH = BL * 8
PIECE = CH

DIRS = (
    (-1, 0), (1, 0), (0, -1), (0, 1), (-1, -1), (-1, 1), (1, -1), (1, 1), (0, -2), (0, 2)
)
OPP = tuple(DIRS.index((-a, -b)) for a, b in DIRS)


def relax_weight(k):
    return 1.0 / (1.4 + 0.6 * math.cos(math.pi * (2 * k + 1) / (2 * ROUNDS)))


def harmonic(a, b):
    return 2.0 * a * b / jnp.maximum(a + b, 1e-30)


def roll_x(v, s):
    return pltpu.roll(v.reshape(v.shape[0] // 8, 8, LANES), s % 8, 1).reshape(v.shape)


def roll_y(v, s):
    return pltpu.roll(v, s % LANES, 1)


def roll_z(v, s):
    return pltpu.roll(v, s % v.shape[0], 0)


def reduce_factors(low, high, roll):
    l, u, d = -low, -high, None
    parts = []
    for s in (1, 2, 4):
        if d is None:
            a, b, d = low, high, jnp.ones_like(low)
        else:
            rd = 1.0 / d
            a, b = -l * roll(rd, s), -u * roll(rd, -s)
        d = d + a * roll(u, s) + b * roll(l, -s)
        l, u = a * roll(l, s), b * roll(u, -s)
        parts += [a, b]
    return parts + [1.0 / d]


def reduce_x(r, f):
    a1, b1, a2, b2, c3, iv = f
    r = r + a1 * roll_x(r, 1) + b1 * roll_x(r, -1)
    r = r + a2 * roll_x(r, 2) + b2 * roll_x(r, -2)
    r = r + c3 * roll_x(r, 4)
    return r * iv


def reduce_y(r, f):
    a1, b1, a2, b2, a3, b3, iv = f
    r = r + a1 * roll_y(r, 1) + b1 * roll_y(r, -1)
    r = r + a2 * roll_y(r, 2) + b2 * roll_y(r, -2)
    r = r + a3 * roll_y(r, 4) + b3 * roll_y(r, -4)
    return r * iv


def col(x, planes=ROWS, first=0):
    return pl.ds(first * 8 + x, planes, stride=8)


def kernel(
    fac_h, fperm_h, pscale_h, src_h, p0_h, depth_h, out,
    fac, pscale, src, p0, fperm, depth, in_sem, gs, gr, c2r, outs, outr, ycf,
    zs, xs, ds, zr, xr, dr, mx, mzr, mxr, mdr, fzr, cs, cr,
    perm, pres, sper, spre, isrc, tgt, tside, e0, e1, e2, ub, corr,
    co, xf, yf, zf, gx, cx, sco, syf,
    i_send, i_recv, m_send, m_recv, f_send, f_recv, g_send, g_recv,
    c_send, c_recv, c2_send, c2_recv, a_send, a_recv,
):
    n_sub, n_grp = lax.axis_size("sub"), lax.axis_size("grp")
    sub, grp = lax.axis_index("sub"), lax.axis_index("grp")
    has_axis = {
        (-1, 0): sub > 0,
        (1, 0): sub < n_sub - 1,
        (0, -1): grp > 0,
        (0, 1): grp < n_grp - 1,
        (0, -2): grp > 1,
        (0, 2): grp < n_grp - 2,
    }
    has = []
    for dz, dx in DIRS:
        if dz and dx:
            has.append(jnp.logical_and(has_axis[(dz, 0)], has_axis[(0, dx)]))
        else:
            has.append(has_axis[(dz, dx)])

    def peer(d):
        return {"sub": sub + DIRS[d][0], "grp": grp + DIRS[d][1]}

    def remote(d, a, b, s_sem, r_sem):
        return pltpu.make_async_remote_copy(
            src_ref=a, dst_ref=b, send_sem=s_sem, recv_sem=r_sem,
            device_id=peer(d), device_id_type=MESH,
        )

    def exchange_start(dirs, make):
        for d in dirs:
            @pl.when(has[d])
            def _(d=d):
                make(d, OPP[d]).start()

    def exchange_wait(dirs, make):
        for d in dirs:
            @pl.when(has[d])
            def _(d=d):
                make(d, d).wait_recv()

    def exchange_sent(dirs, makes):
        for d in dirs:
            @pl.when(has[d])
            def _(d=d):
                for make in makes:
                    make(d, OPP[d]).wait_send()

    barrier = pltpu.get_barrier_semaphore()
    for d in range(len(DIRS)):
        @pl.when(has[d])
        def _(d=d):
            pl.semaphore_signal(barrier, inc=1, device_id=peer(d), device_id_type=MESH)

    loads = [
        pltpu.make_async_copy(a, b, in_sem.at[i])
        for i, (a, b) in enumerate((
            (fac_h, fac), (pscale_h, pscale), (p0_h, p0), (src_h, src),
            (fperm_h, fperm), (depth_h, depth),
        ))
    ]
    for load in loads:
        load.start()

    for d in range(len(DIRS)):
        @pl.when(jnp.logical_not(has[d]))
        def _(d=d):
            if d < 2:
                zr[d] = jnp.zeros(zr.shape[1:], jnp.float32)
                mzr[d] = jnp.zeros(mzr.shape[1:], jnp.float32)
                fzr[d] = jnp.zeros(fzr.shape[1:], jnp.float32)
            elif d < 4:
                xr[d - 2] = jnp.zeros(xr.shape[1:], jnp.float32)
                mxr[d - 2] = jnp.zeros(mxr.shape[1:], jnp.float32)
                gr[d - 2] = jnp.zeros(gr.shape[1:], jnp.float32)
                for ph in range(cr.shape[0]):
                    cr[ph, d - 2] = jnp.zeros(cr.shape[2:], jnp.float32)
                    outr[ph, d - 2] = jnp.zeros(outr.shape[2:], jnp.float32)
            elif d < 8:
                dr[d - 4] = jnp.zeros(dr.shape[1:], jnp.float32)
                mdr[d - 4] = jnp.zeros(mdr.shape[1:], jnp.float32)
            else:
                for ph in range(c2r.shape[0]):
                    c2r[ph, d - 8] = jnp.zeros(c2r.shape[2:], jnp.float32)

    for i in (0, 1, 4):
        loads[i].wait()
    kinds = fac[...]
    own = jnp.zeros(kinds.shape, jnp.float32)
    for kind in range(FACIES):
        own = jnp.where(kinds == kind, fperm[kind], own)
    perm[pl.ds(40, OWN * 8)] = (own * pscale[...]).reshape(OWN * 8, LANES)
    for s in range(2):
        near, far = (0, 1) if s == 0 else (7, 6)
        zs[s, pl.ds(0, 40)] = perm[pl.ds(40 if s == 0 else 128, 40)]
        xs[s, pl.ds(0, 16)] = perm[col(near, 16, 5)]
        xs[s, pl.ds(16, 16)] = perm[col(far, 16, 5)]
        for z in range(2):
            at_rows = 5 if z == 0 else 13
            ds[2 * z + s, pl.ds(0, 8)] = perm[col(near, 8, at_rows)]
            ds[2 * z + s, pl.ds(8, 8)] = perm[col(far, 8, at_rows)]

    def init_copy(part):
        def make(d, slot):
            if d < 2:
                at, a, b = (pl.ds(0, 40), pl.ds(40, 72))[part], zs.at[d], zr.at[slot]
            elif d < 4:
                at, a, b = (pl.ds(0, 32), pl.ds(32, 16))[part], xs.at[d - 2], xr.at[slot - 2]
            else:
                at, a, b = (pl.ds(0, 16), pl.ds(16, 8))[part], ds.at[d - 4], dr.at[slot - 4]
            return remote(d, a.at[at], b.at[at], i_send.at[part, d], i_recv.at[part, slot])
        return make

    pl.semaphore_wait(barrier, sum(jnp.where(h, 1, 0) for h in has))
    exchange_start(range(8), init_copy(0))
    for i in (2, 3, 5):
        loads[i].wait()
    pres[pl.ds(40, OWN * 8)] = p0[...].reshape(OWN * 8, LANES)
    isrc[pl.ds(32, OWN * 8)] = src[...].reshape(OWN * 8, LANES)
    for s in range(2):
        near = 7 * s
        zs[s, pl.ds(40, 40)] = pres[pl.ds(40 if s == 0 else 128, 40)]
        zs[s, pl.ds(80, 32)] = isrc[pl.ds(32 if s == 0 else 128, 32)]
        xs[s, pl.ds(32, 16)] = pres[col(near, 16, 5)]
        for z in range(2):
            ds[2 * z + s, pl.ds(16, 8)] = pres[col(near, 8, 5 if z == 0 else 13)]
    exchange_start(range(8), init_copy(1))

    low = jnp.where(sub > 0, depth[jnp.maximum(sub - 1, 0)], 0)
    high = jnp.where(sub < n_sub - 1, depth[jnp.minimum(sub, n_sub - 2)], 0)

    def active(rows):
        inside = (rows >= OV - low) & (rows < OV + OWN + high)
        return jnp.where(inside, 1.0, 0.0)

    def rows_of(c):
        return lax.broadcasted_iota(jnp.int32, (8, 8, LANES), 0).reshape(CH, LANES) + 8 * c

    lane = lax.broadcasted_iota(jnp.int32, (CH, LANES), 1)
    lane2 = lax.broadcasted_iota(jnp.int32, (ROWS, LANES), 1)
    row2 = lax.broadcasted_iota(jnp.int32, (ROWS, LANES), 0)
    subl = lax.broadcasted_iota(jnp.int32, (8, 8, LANES), 1).reshape(CH, LANES)
    zeros_plane = jnp.zeros((8, LANES), jnp.float32)
    for e in (e0, e1, e2):
        e[pl.ds(0, 8)] = zeros_plane
        e[pl.ds((ROWS + 1) * 8, 8)] = zeros_plane

    exchange_wait(range(8), init_copy(0))
    perm[pl.ds(0, 40)] = zr[0, pl.ds(0, 40)]
    perm[pl.ds(168, 40)] = zr[1, pl.ds(0, 40)]
    for s in range(2):
        for f in range(2):
            sper[s, f, pl.ds(5, 16)] = xr[s, pl.ds(16 * f, 16)]
            sper[s, f, pl.ds(0, 5)] = dr[s, pl.ds(8 * f + 3, 5)]
            sper[s, f, pl.ds(21, 5)] = dr[2 + s, pl.ds(8 * f, 5)]
        ub[col(7 * s)] = sper[s, 0, pl.ds(1, ROWS)]

    for c in range(CHUNKS):
        here = pl.ds(c * CH, CH)
        mid = perm[pl.ds((c * 8 + 1) * 8, CH)]
        edge = ub[here]
        fb = harmonic(perm[pl.ds(c * CH, CH)], mid)
        fa = harmonic(mid, perm[pl.ds((c * 8 + 2) * 8, CH)])
        fl = harmonic(jnp.where(subl == 0, edge, roll_x(mid, 1)), mid)
        fr = harmonic(mid, jnp.where(subl == 7, edge, roll_x(mid, -1)))
        ff = harmonic(jnp.where(lane == 0, 0.0, roll_y(mid, 1)), mid)
        fk = harmonic(mid, jnp.where(lane == LANES - 1, 0.0, roll_y(mid, -1)))
        act = active(rows_of(c))
        inv = act / (STORE + fb + fa + fl + fr + ff + fk)
        fl, fr = fl * inv, fr * inv
        ub[here] = jnp.where(subl == 0, fl, fr)
        fl, fr = jnp.where(subl == 0, 0.0, fl), jnp.where(subl == 7, 0.0, fr)
        fb, fa, ff, fk = fb * inv, fa * inv, ff * inv, fk * inv
        for i, f in enumerate((fb, fa, fl, fr, ff, fk)):
            co[i, here] = f
        zf[0, here] = inv
        a1, b1, a2, b2, a3, b3, iv = reduce_factors(fl, fr, roll_x)
        for i, f in enumerate((a2, b2, a3 + b3, iv)):
            xf[i, here] = f
    for s in range(2):
        cx[s] = ub[col(7 * s)]

    def xfac(here):
        return [co[2, here], co[3, here]] + [xf[i, here] for i in range(4)]

    exchange_wait(range(8), init_copy(1))
    pres[pl.ds(0, 40)] = zr[0, pl.ds(40, 40)]
    isrc[pl.ds(0, 32)] = zr[0, pl.ds(80, 32)]
    pres[pl.ds(168, 40)] = zr[1, pl.ds(40, 40)]
    isrc[pl.ds(160, 32)] = zr[1, pl.ds(80, 32)]
    isrc[...] = isrc[...] * zf[0]
    for s in range(2):
        spre[s, pl.ds(4, 16)] = xr[s, pl.ds(32, 16)]
        spre[s, pl.ds(0, 4)] = dr[s, pl.ds(20, 4)]
        spre[s, pl.ds(20, 4)] = dr[2 + s, pl.ds(16, 4)]
    for c in range(CHUNKS):
        gx[0, pl.ds(c * CH, CH)] = ub[pl.ds(c * CH, CH)]
        ub[pl.ds(c * CH, CH)] = jnp.zeros((CH, LANES), jnp.float32)

    def answer_copy(d, slot):
        return remote(
            d, gs.at[d - 2], gr.at[slot - 2], g_send.at[d - 2], g_recv.at[slot - 2]
        )

    def rest_of_setup():
        for c in range(CHUNKS):
            here = pl.ds(c * CH, CH)
            fb, fa, ff, fk = (co[i, here] for i in (0, 1, 4, 5))
            fy = reduce_factors(
                jnp.where(lane % BL == 0, 0.0, ff), jnp.where(lane % BL == BL - 1, 0.0, fk), roll_y
            )
            for i, f in enumerate(fy):
                yf[i, here] = f
            lz = -fb * active(rows_of(c) - 1)
            uz = -fa * active(rows_of(c) + 1)
            d = None
            for i in range(BL):
                at = pl.ds(c * CH + i * 8, 8)
                part = slice(i * 8, i * 8 + 8)
                if i == 0:
                    m, d = zeros_plane, jnp.ones((8, LANES), jnp.float32)
                else:
                    m = lz[part] / d
                    d = 1.0 - m * uz[(i - 1) * 8 : i * 8]
                zf[0, at] = m
                zf[1, at] = 1.0 / d
                zf[2, at] = uz[part] / d
        for c in range(CHUNKS):
            here = pl.ds(c * CH, CH)
            edge, f = gx[0, here], xfac(here)
            for s in range(2):
                gx[s, here] = reduce_x(jnp.where(subl == 7 * s, edge, 0.0), f)
        for s in range(2):
            near, far = (0, 1) if s == 0 else (7, 6)
            for i in range(2):
                gs[s, pl.ds(2 * i * ROWS, ROWS)] = gx[i, col(near)]
                gs[s, pl.ds((2 * i + 1) * ROWS, ROWS)] = gx[i, col(far)]

        exchange_start((2, 3), answer_copy)

        for s in range(2):
            for i in range(7):
                ycf[s, i] = yf[i, col(7 * s)]

        for s in range(2):
            mid = sper[s, 0, pl.ds(1, ROWS)]
            fb = harmonic(sper[s, 0, pl.ds(0, ROWS)], mid)
            fa = harmonic(mid, sper[s, 0, pl.ds(2, ROWS)])
            fx = harmonic(mid, sper[s, 1, pl.ds(1, ROWS)])
            fo = harmonic(mid, perm[col(7 * s, ROWS, 1)])
            ff = harmonic(jnp.where(lane2 == 0, 0.0, roll_y(mid, 1)), mid)
            fk = harmonic(mid, jnp.where(lane2 == LANES - 1, 0.0, roll_y(mid, -1)))
            inv = active(row2) / (STORE + fb + fa + fx + fo + ff + fk)
            fb = jnp.where(row2 == 0, 0.0, fb * inv)
            fa = jnp.where(row2 == ROWS - 1, 0.0, fa * inv)
            ff, fk = ff * inv, fk * inv
            for i, f in enumerate((fb, fa, fx * inv, fo * inv, ff, fk)):
                sco[s, i] = f
            fy = reduce_factors(
                jnp.where(lane2 % BL == 0, 0.0, ff), jnp.where(lane2 % BL == BL - 1, 0.0, fk), roll_y
            )
            for i, f in enumerate(fy):
                syf[s, i] = f

    def update(t, e, at, scale=None):
        here = pl.ds(at, PIECE)
        v = e[pl.ds(at + 8, PIECE)]
        u = t[here] - (v if scale is None else v * scale)
        u = u + co[0, here] * e[here] + co[1, here] * e[pl.ds(at + 16, PIECE)]
        u = u + co[2, here] * roll_x(v, 1) + co[3, here] * roll_x(v, -1)
        return v, u + co[4, here] * roll_y(v, 1) + co[5, here] * roll_y(v, -1)

    def col_copy(ph, rows):
        def make(d, slot):
            return remote(
                d, cs.at[ph, d - 2, pl.ds(0, rows)], cr.at[ph, slot - 2, pl.ds(0, rows)],
                c_send.at[ph, d - 2], c_recv.at[ph, slot - 2],
            )
        return make

    def solved_copy(ph):
        def make(d, slot):
            if d < 4:
                return remote(
                    d, outs.at[ph, d - 2], outr.at[ph, slot - 2],
                    a_send.at[ph, d - 2], a_recv.at[ph, slot - 2],
                )
            return remote(
                d, outs.at[ph, d - 8], c2r.at[ph, slot - 8],
                c2_send.at[ph, d - 8], c2_recv.at[ph, slot - 8],
            )
        return make

    def one_round(outer, k):
        first = isinstance(k, int)
        ph = outer * ROUNDS + k
        om = relax_weight(0)
        if not first:
            for i in range(1, ROUNDS):
                om = jnp.where(k == i, jnp.float32(relax_weight(i)), om)
        for at in range(0, ROWS * 8, PIECE):
            here = pl.ds(at, PIECE)
            if first:
                e1[pl.ds(at + 8, PIECE)] = om * reduce_x(tgt[here], xfac(here))
            else:
                v, u = update(tgt, e0, at)
                e1[pl.ds(at + 8, PIECE)] = v + om * reduce_x(u, xfac(here))
        for s in range(2):
            near, far = (0, 1) if s == 0 else (7, 6)
            cs[ph, s, pl.ds(0, ROWS)] = e1[col(near, ROWS, 1)]
            cs[ph, s, pl.ds(ROWS, ROWS)] = e1[col(far, ROWS, 1)]
            if first:
                cs[ph, s, pl.ds(2 * ROWS, ROWS)] = tgt[col(near)]
        make = col_copy(ph, (3 if first else 2) * ROWS)
        exchange_start((2, 3), make)
        if first:
            pl.when(outer == 0)(rest_of_setup)
        if not first:
            exchange_wait((2, 3, 8, 9), solved_copy(ph))
            for z in range(ROWS):
                at, here = pl.ds((z + 1) * 8, 8), pl.ds(z * 8, 8)
                left = jnp.broadcast_to(outr[ph, 0, pl.ds(z, 1)], (8, LANES))
                right = jnp.broadcast_to(outr[ph, 1, pl.ds(z, 1)], (8, LANES))
                e1[at] = e1[at] + om * (gx[0, here] * left + gx[1, here] * right)
        for at in range(0, ROWS * 8, PIECE):
            here = pl.ds(at, PIECE)
            v, u = update(tgt, e1, at)
            e2[pl.ds(at + 8, PIECE)] = v + om * reduce_y(u, [yf[i, here] for i in range(7)])
        exchange_wait((2, 3), make)
        for s in range(2):
            near, far = cr[ph, s, pl.ds(0, ROWS)], cr[ph, s, pl.ds(ROWS, ROWS)]
            if first:
                tside[s] = cr[ph, s, pl.ds(2 * ROWS, ROWS)]
            else:
                beyond, inner = c2r[ph, s], e0[col(7 * s, ROWS, 1)]
                left, right = (beyond, inner) if s == 0 else (inner, beyond)
                g = [gr[s, pl.ds(i * ROWS, ROWS)] for i in range(4)]
                near = near + om * (g[0] * left + g[2] * right)
                far = far + om * (g[1] * left + g[3] * right)
            u = tside[s] - near
            u = u + sco[s, 0] * roll_z(near, 1) + sco[s, 1] * roll_z(near, -1)
            u = u + sco[s, 2] * far + sco[s, 3] * e1[col(7 * s, ROWS, 1)]
            u = u + sco[s, 4] * roll_y(near, 1) + sco[s, 5] * roll_y(near, -1)
            beside = near + om * reduce_y(u, [syf[s, i] for i in range(7)])
            ub[col(7 * s)] = cx[s] * beside
            at = col(7 * s, ROWS, 1)
            e2[at] = e2[at] + om * reduce_y(cx[s] * near, [ycf[s, i] for i in range(7)])
        for at in range(0, ROWS * 8, PIECE):
            v, u = update(tgt, e2, at)
            u = (u + ub[pl.ds(at, PIECE)]).reshape(PIECE // CH, BL, 8, LANES)
            m, iv, up = (zf[i, pl.ds(at, PIECE)].reshape(u.shape) for i in range(3))
            v = v.reshape(u.shape)
            fw = [u[:, 0]]
            for i in range(1, BL):
                fw.append(u[:, i] - m[:, i] * fw[-1])
            nxt = None
            for i in range(BL - 1, -1, -1):
                x = fw[i] * iv[:, i]
                nxt = x if nxt is None else x - up[:, i] * nxt
                new = v[:, i] + om * nxt
                for c in range(PIECE // CH):
                    e0[pl.ds(at + c * CH + (i + 1) * 8, 8)] = new[c]

        def send_next():
            for s in range(2):
                outs[ph + 1, s] = e0[col(7 * s, ROWS, 1)]
            exchange_start((2, 3, 8, 9), solved_copy(ph + 1))

        if first:
            send_next()
        else:
            pl.when(k < ROUNDS - 1)(send_next)

    def mid_copy(d, slot):
        if d < 2:
            a, b = corr.at[pl.ds(0 if d == 0 else 120, 72)], mzr.at[slot]
        elif d < 4:
            a, b = mx.at[d - 2], mxr.at[slot - 2]
        else:
            z, s = divmod(d - 4, 2)
            a, b = mx.at[s, pl.ds(16 * z, 8)], mdr.at[slot - 4]
        return remote(d, a, b, m_send.at[d], m_recv.at[slot])

    def end_copy(d, slot):
        a = corr.at[pl.ds(0 if d == 0 else 160, 32)]
        return remote(d, a, fzr.at[slot], f_send.at[d], f_recv.at[slot])

    def iteration(outer, carry):
        for s in range(2):
            ub[col(7 * s)] = cx[s] * spre[s]
        for c in range(0, CHUNKS, PIECE // CH):
            rows = [active(rows_of(i)) for i in range(c, c + PIECE // CH)]
            here = pl.ds(c * CH, PIECE)
            tgt[here] = update(isrc, pres, c * CH, jnp.concatenate(rows))[1] + ub[here]
        one_round(outer, 0)

        @pl.when(outer == 0)
        def _():
            exchange_wait((2, 3), answer_copy)

        def step(k, carry):
            one_round(outer, k)
            return carry

        lax.fori_loop(1, ROUNDS, step, 0)

        @pl.when(outer == 1)
        def _():
            exchange_sent(range(8), [mid_copy])

        for c in range(CHUNKS):
            rows = rows_of(c)
            band = (rows < OV + low) | (rows >= OV + OWN - high)
            w = active(rows) * jnp.where(band, 0.5, 1.0)
            corr[pl.ds(c * CH, CH)] = w * e0[pl.ds((c * 8 + 1) * 8, CH)]

        @pl.when(outer == 0)
        def _():
            for s in range(2):
                mx[s] = corr[col(7 * s)]
            exchange_start(range(8), mid_copy)
            pres[pl.ds(8, ROWS * 8)] = pres[pl.ds(8, ROWS * 8)] + corr[...]
            exchange_wait(range(8), mid_copy)
            for z in range(2):
                at = pl.ds(0 if z == 0 else 17 * 8, 72)
                pres[at] = pres[at] + mzr[z]
            for s in range(2):
                spre[s] = spre[s] + mxr[s]
                for z in range(2):
                    at = pl.ds(16 * z, 8)
                    spre[s, at] = spre[s, at] + mdr[2 * z + s]

        @pl.when(outer == 1)
        def _():
            exchange_start((0, 1), end_copy)
            later = [k for k in range(OUTER * ROUNDS) if k % ROUNDS]
            exchange_sent(range(8), [init_copy(0), init_copy(1)])
            makes = [col_copy(k, (2 if k % ROUNDS else 3) * ROWS) for k in range(OUTER * ROUNDS)]
            makes += [solved_copy(k) for k in later]
            exchange_sent((2, 3), makes + [answer_copy])
            exchange_sent((8, 9), [solved_copy(k) for k in later])
            exchange_sent((0, 1), [end_copy])
            pres[pl.ds(8, ROWS * 8)] = pres[pl.ds(8, ROWS * 8)] + corr[...]
            exchange_wait((0, 1), end_copy)
            for z in range(2):
                at = pl.ds(40 if z == 0 else 17 * 8, 32)
                pres[at] = pres[at] + fzr[z]
        return carry

    lax.fori_loop(0, OUTER, iteration, 0)
    out[...] = pres[pl.ds(40, OWN * 8)].reshape(OWN, 8, LANES)


def on_device(facies, facies_perm, perm_scale, source, pressure_start, intersection_depth):
    assert source.shape == (OWN, 8, LANES)
    f32 = jnp.float32

    def buf(*shape):
        return pltpu.VMEM(shape, f32)

    field, wide = (ROWS * 8, LANES), (WIDE * 8, LANES)
    phases, own, dma = OUTER * ROUNDS, source.shape, pltpu.SemaphoreType.DMA
    scratch = [
        pltpu.VMEM(own, jnp.int32), buf(*own), buf(*own), buf(*own),
        pltpu.SMEM(facies_perm.shape, f32), pltpu.SMEM(intersection_depth.shape, jnp.int32),
        dma((6,)), buf(2, 4 * ROWS, LANES), buf(2, 4 * ROWS, LANES),
        *[buf(phases, 2, ROWS, LANES)] * 3, buf(2, 7, ROWS, LANES),
        buf(2, 112, LANES), buf(2, 48, LANES), buf(4, 24, LANES),
        buf(2, 112, LANES), buf(2, 48, LANES), buf(4, 24, LANES),
        buf(2, ROWS, LANES), buf(2, 72, LANES), buf(2, ROWS, LANES), buf(4, 8, LANES),
        buf(2, 32, LANES), buf(phases, 2, 3 * ROWS, LANES), buf(phases, 2, 3 * ROWS, LANES),
        buf(*wide), buf(*wide), buf(2, 2, 32, LANES), buf(2, ROWS, LANES),
        buf(*field), buf(*field), buf(2, ROWS, LANES),
        buf(*wide), buf(*wide), buf(*wide), buf(*field), buf(*field),
        buf(6, *field), buf(4, *field), buf(7, *field), buf(3, *field),
        buf(2, *field), buf(2, ROWS, LANES), buf(2, 6, ROWS, LANES), buf(2, 7, ROWS, LANES),
    ]
    sems = [dma((2, 8)), dma((2, 8))] + [dma((n,)) for n in (8, 8, 2, 2, 2, 2)]
    sems += [dma((phases, 2)) for _ in range(6)]
    return pl.pallas_call(
        kernel,
        out_shape=jax.ShapeDtypeStruct(source.shape, f32),
        in_specs=[pl.BlockSpec(memory_space=pltpu.HBM)] * 6,
        out_specs=pl.BlockSpec(memory_space=pltpu.VMEM),
        scratch_shapes=scratch + sems,
        compiler_params=pltpu.CompilerParams(
            collective_id=0, has_side_effects=True, vmem_limit_bytes=60 * 1024 * 1024
        ),
        name="schwarz",
    )(facies, facies_perm, perm_scale, source, pressure_start, intersection_depth)


def solution(mesh):
    return jax.shard_map(
        on_device,
        mesh=mesh,
        in_specs=(
            P("sub", "grp", None),
            P(),
            P("sub", "grp", None),
            P("sub", "grp", None),
            P("sub", "grp", None),
            P(),
        ),
        out_specs=P("sub", "grp", None),
        check_vma=False,
    )
```

```python
import functools
import math

import jax
import jax.numpy as jnp
from jax import lax
from jax.experimental import pallas as pl
from jax.experimental.pallas import tpu as pltpu
from jax.sharding import PartitionSpec as P

OV = 4
BL = 8
ROUNDS = 4
OUTER = 2
FACIES = 8
STORE = 0.02
MESH = pl.DeviceIdType.MESH

OWN = 16
ROWS = OWN + 2 * OV
WIDE = ROWS + 2
LANES = 128
CHUNKS = ROWS // BL
CH = BL * 8
PIECE = CH

DIRS = (
    (-1, 0), (1, 0), (0, -1), (0, 1), (-1, -1), (-1, 1), (1, -1), (1, 1), (0, -2), (0, 2)
)
OPP = tuple(DIRS.index((-a, -b)) for a, b in DIRS)


def relax_weight(k):
    return 1.0 / (1.4 + 0.6 * math.cos(math.pi * (2 * k + 1) / (2 * ROUNDS)))


def harmonic(a, b):
    return 2.0 * a * b / jnp.maximum(a + b, 1e-30)


def roll_x(v, s):
    return pltpu.roll(v.reshape(v.shape[0] // 8, 8, LANES), s % 8, 1).reshape(v.shape)


def roll_y(v, s):
    return pltpu.roll(v, s % LANES, 1)


def roll_z(v, s):
    return pltpu.roll(v, s % v.shape[0], 0)


def reduce_factors(low, high, roll):
    l, u, d = -low, -high, None
    parts = []
    for s in (1, 2, 4):
        if d is None:
            a, b, d = low, high, jnp.ones_like(low)
        else:
            rd = 1.0 / d
            a, b = -l * roll(rd, s), -u * roll(rd, -s)
        d = d + a * roll(u, s) + b * roll(l, -s)
        l, u = a * roll(l, s), b * roll(u, -s)
        parts += [a, b]
    return parts + [1.0 / d]


def reduce_x(r, f):
    a1, b1, a2, b2, c3, iv = f
    r = r + a1 * roll_x(r, 1) + b1 * roll_x(r, -1)
    r = r + a2 * roll_x(r, 2) + b2 * roll_x(r, -2)
    r = r + c3 * roll_x(r, 4)
    return r * iv


def reduce_y(r, f):
    a1, b1, a2, b2, a3, b3, iv = f
    r = r + a1 * roll_y(r, 1) + b1 * roll_y(r, -1)
    r = r + a2 * roll_y(r, 2) + b2 * roll_y(r, -2)
    r = r + a3 * roll_y(r, 4) + b3 * roll_y(r, -4)
    return r * iv


def col(x, planes=ROWS, first=0):
    return pl.ds(first * 8 + x, planes, stride=8)


def kernel(
    fac_h, fperm_h, pscale_h, src_h, p0_h, depth_h, out,
    fac, pscale, src, p0, fperm, depth, in_sem, gs, gr, c2r, outs, outr, ycf,
    zs, xs, ds, zr, xr, dr, mx, mzr, mxr, mdr, fzr, cs, cr,
    perm, pres, sper, spre, isrc, tgt, tside, e0, e1, e2, ub, corr,
    co, xf, yf, zf, gx, cx, sco, syf,
    i_send, i_recv, m_send, m_recv, f_send, f_recv, g_send, g_recv,
    c_send, c_recv, c2_send, c2_recv, a_send, a_recv,
):
    n_sub, n_grp = lax.axis_size("sub"), lax.axis_size("grp")
    sub, grp = lax.axis_index("sub"), lax.axis_index("grp")
    has_axis = {
        (-1, 0): sub > 0,
        (1, 0): sub < n_sub - 1,
        (0, -1): grp > 0,
        (0, 1): grp < n_grp - 1,
        (0, -2): grp > 1,
        (0, 2): grp < n_grp - 2,
    }
    has = []
    for dz, dx in DIRS:
        if dz and dx:
            has.append(jnp.logical_and(has_axis[(dz, 0)], has_axis[(0, dx)]))
        else:
            has.append(has_axis[(dz, dx)])

    def peer(d):
        return {"sub": sub + DIRS[d][0], "grp": grp + DIRS[d][1]}

    def remote(d, a, b, s_sem, r_sem):
        return pltpu.make_async_remote_copy(
            src_ref=a, dst_ref=b, send_sem=s_sem, recv_sem=r_sem,
            device_id=peer(d), device_id_type=MESH,
        )

    def exchange_start(dirs, make):
        for d in dirs:
            @pl.when(has[d])
            def _(d=d):
                make(d, OPP[d]).start()

    def exchange_wait(dirs, make):
        for d in dirs:
            @pl.when(has[d])
            def _(d=d):
                make(d, d).wait_recv()

    def exchange_sent(dirs, makes):
        for d in dirs:
            @pl.when(has[d])
            def _(d=d):
                for make in makes:
                    make(d, OPP[d]).wait_send()

    barrier = pltpu.get_barrier_semaphore()
    for d in range(len(DIRS)):
        @pl.when(has[d])
        def _(d=d):
            pl.semaphore_signal(barrier, inc=1, device_id=peer(d), device_id_type=MESH)

    loads = [
        pltpu.make_async_copy(a, b, in_sem.at[i])
        for i, (a, b) in enumerate((
            (fac_h, fac), (pscale_h, pscale), (p0_h, p0), (src_h, src),
            (fperm_h, fperm), (depth_h, depth),
        ))
    ]
    for load in loads:
        load.start()

    for d in range(len(DIRS)):
        @pl.when(jnp.logical_not(has[d]))
        def _(d=d):
            if d < 2:
                zr[d] = jnp.zeros(zr.shape[1:], jnp.float32)
                mzr[d] = jnp.zeros(mzr.shape[1:], jnp.float32)
                fzr[d] = jnp.zeros(fzr.shape[1:], jnp.float32)
            elif d < 4:
                xr[d - 2] = jnp.zeros(xr.shape[1:], jnp.float32)
                mxr[d - 2] = jnp.zeros(mxr.shape[1:], jnp.float32)
                gr[d - 2] = jnp.zeros(gr.shape[1:], jnp.float32)
                for ph in range(cr.shape[0]):
                    cr[ph, d - 2] = jnp.zeros(cr.shape[2:], jnp.float32)
                    outr[ph, d - 2] = jnp.zeros(outr.shape[2:], jnp.float32)
            elif d < 8:
                dr[d - 4] = jnp.zeros(dr.shape[1:], jnp.float32)
                mdr[d - 4] = jnp.zeros(mdr.shape[1:], jnp.float32)
            else:
                for ph in range(c2r.shape[0]):
                    c2r[ph, d - 8] = jnp.zeros(c2r.shape[2:], jnp.float32)

    for i in (0, 1, 4):
        loads[i].wait()
    kinds = fac[...]
    own = jnp.zeros(kinds.shape, jnp.float32)
    for kind in range(FACIES):
        own = jnp.where(kinds == kind, fperm[kind], own)
    perm[pl.ds(40, OWN * 8)] = (own * pscale[...]).reshape(OWN * 8, LANES)
    for s in range(2):
        near, far = (0, 1) if s == 0 else (7, 6)
        zs[s, pl.ds(0, 40)] = perm[pl.ds(40 if s == 0 else 128, 40)]
        xs[s, pl.ds(0, 16)] = perm[col(near, 16, 5)]
        xs[s, pl.ds(16, 16)] = perm[col(far, 16, 5)]
        for z in range(2):
            at_rows = 5 if z == 0 else 13
            ds[2 * z + s, pl.ds(0, 8)] = perm[col(near, 8, at_rows)]
            ds[2 * z + s, pl.ds(8, 8)] = perm[col(far, 8, at_rows)]

    def init_copy(part):
        def make(d, slot):
            if d < 2:
                at, a, b = (pl.ds(0, 40), pl.ds(40, 72))[part], zs.at[d], zr.at[slot]
            elif d < 4:
                at, a, b = (pl.ds(0, 32), pl.ds(32, 16))[part], xs.at[d - 2], xr.at[slot - 2]
            else:
                at, a, b = (pl.ds(0, 16), pl.ds(16, 8))[part], ds.at[d - 4], dr.at[slot - 4]
            return remote(d, a.at[at], b.at[at], i_send.at[part, d], i_recv.at[part, slot])
        return make

    pl.semaphore_wait(barrier, sum(jnp.where(h, 1, 0) for h in has))
    exchange_start(range(8), init_copy(0))
    for i in (2, 3, 5):
        loads[i].wait()
    pres[pl.ds(40, OWN * 8)] = p0[...].reshape(OWN * 8, LANES)
    isrc[pl.ds(32, OWN * 8)] = src[...].reshape(OWN * 8, LANES)
    for s in range(2):
        near = 7 * s
        zs[s, pl.ds(40, 40)] = pres[pl.ds(40 if s == 0 else 128, 40)]
        zs[s, pl.ds(80, 32)] = isrc[pl.ds(32 if s == 0 else 128, 32)]
        xs[s, pl.ds(32, 16)] = pres[col(near, 16, 5)]
        for z in range(2):
            ds[2 * z + s, pl.ds(16, 8)] = pres[col(near, 8, 5 if z == 0 else 13)]
    exchange_start(range(8), init_copy(1))

    low = jnp.where(sub > 0, depth[jnp.maximum(sub - 1, 0)], 0)
    high = jnp.where(sub < n_sub - 1, depth[jnp.minimum(sub, n_sub - 2)], 0)

    def active(rows):
        inside = (rows >= OV - low) & (rows < OV + OWN + high)
        return jnp.where(inside, 1.0, 0.0)

    def rows_of(c):
        return lax.broadcasted_iota(jnp.int32, (8, 8, LANES), 0).reshape(CH, LANES) + 8 * c

    lane = lax.broadcasted_iota(jnp.int32, (CH, LANES), 1)
    lane2 = lax.broadcasted_iota(jnp.int32, (ROWS, LANES), 1)
    row2 = lax.broadcasted_iota(jnp.int32, (ROWS, LANES), 0)
    subl = lax.broadcasted_iota(jnp.int32, (8, 8, LANES), 1).reshape(CH, LANES)
    zeros_plane = jnp.zeros((8, LANES), jnp.float32)
    for e in (e0, e1, e2):
        e[pl.ds(0, 8)] = zeros_plane
        e[pl.ds((ROWS + 1) * 8, 8)] = zeros_plane

    exchange_wait(range(8), init_copy(0))
    perm[pl.ds(0, 40)] = zr[0, pl.ds(0, 40)]
    perm[pl.ds(168, 40)] = zr[1, pl.ds(0, 40)]
    for s in range(2):
        for f in range(2):
            sper[s, f, pl.ds(5, 16)] = xr[s, pl.ds(16 * f, 16)]
            sper[s, f, pl.ds(0, 5)] = dr[s, pl.ds(8 * f + 3, 5)]
            sper[s, f, pl.ds(21, 5)] = dr[2 + s, pl.ds(8 * f, 5)]
        ub[col(7 * s)] = sper[s, 0, pl.ds(1, ROWS)]

    for c in range(CHUNKS):
        here = pl.ds(c * CH, CH)
        mid = perm[pl.ds((c * 8 + 1) * 8, CH)]
        edge = ub[here]
        fb = harmonic(perm[pl.ds(c * CH, CH)], mid)
        fa = harmonic(mid, perm[pl.ds((c * 8 + 2) * 8, CH)])
        fl = harmonic(jnp.where(subl == 0, edge, roll_x(mid, 1)), mid)
        fr = harmonic(mid, jnp.where(subl == 7, edge, roll_x(mid, -1)))
        ff = harmonic(jnp.where(lane == 0, 0.0, roll_y(mid, 1)), mid)
        fk = harmonic(mid, jnp.where(lane == LANES - 1, 0.0, roll_y(mid, -1)))
        act = active(rows_of(c))
        inv = act / (STORE + fb + fa + fl + fr + ff + fk)
        fl, fr = fl * inv, fr * inv
        ub[here] = jnp.where(subl == 0, fl, fr)
        fl, fr = jnp.where(subl == 0, 0.0, fl), jnp.where(subl == 7, 0.0, fr)
        fb, fa, ff, fk = fb * inv, fa * inv, ff * inv, fk * inv
        for i, f in enumerate((fb, fa, fl, fr, ff, fk)):
            co[i, here] = f
        zf[0, here] = inv
        a1, b1, a2, b2, a3, b3, iv = reduce_factors(fl, fr, roll_x)
        for i, f in enumerate((a2, b2, a3 + b3, iv)):
            xf[i, here] = f
    for s in range(2):
        cx[s] = ub[col(7 * s)]

    def xfac(here):
        return [co[2, here], co[3, here]] + [xf[i, here] for i in range(4)]

    exchange_wait(range(8), init_copy(1))
    pres[pl.ds(0, 40)] = zr[0, pl.ds(40, 40)]
    isrc[pl.ds(0, 32)] = zr[0, pl.ds(80, 32)]
    pres[pl.ds(168, 40)] = zr[1, pl.ds(40, 40)]
    isrc[pl.ds(160, 32)] = zr[1, pl.ds(80, 32)]
    isrc[...] = isrc[...] * zf[0]
    for s in range(2):
        spre[s, pl.ds(4, 16)] = xr[s, pl.ds(32, 16)]
        spre[s, pl.ds(0, 4)] = dr[s, pl.ds(20, 4)]
        spre[s, pl.ds(20, 4)] = dr[2 + s, pl.ds(16, 4)]
    for c in range(CHUNKS):
        gx[0, pl.ds(c * CH, CH)] = ub[pl.ds(c * CH, CH)]
        ub[pl.ds(c * CH, CH)] = jnp.zeros((CH, LANES), jnp.float32)

    def answer_copy(d, slot):
        return remote(
            d, gs.at[d - 2], gr.at[slot - 2], g_send.at[d - 2], g_recv.at[slot - 2]
        )

    def rest_of_setup():
        for c in range(CHUNKS):
            here = pl.ds(c * CH, CH)
            fb, fa, ff, fk = (co[i, here] for i in (0, 1, 4, 5))
            fy = reduce_factors(
                jnp.where(lane % BL == 0, 0.0, ff), jnp.where(lane % BL == BL - 1, 0.0, fk), roll_y
            )
            for i, f in enumerate(fy):
                yf[i, here] = f
            lz = -fb * active(rows_of(c) - 1)
            uz = -fa * active(rows_of(c) + 1)
            d = None
            for i in range(BL):
                at = pl.ds(c * CH + i * 8, 8)
                part = slice(i * 8, i * 8 + 8)
                if i == 0:
                    m, d = zeros_plane, jnp.ones((8, LANES), jnp.float32)
                else:
                    m = lz[part] / d
                    d = 1.0 - m * uz[(i - 1) * 8 : i * 8]
                zf[0, at] = m
                zf[1, at] = 1.0 / d
                zf[2, at] = uz[part] / d
        for c in range(CHUNKS):
            here = pl.ds(c * CH, CH)
            edge, f = gx[0, here], xfac(here)
            for s in range(2):
                gx[s, here] = reduce_x(jnp.where(subl == 7 * s, edge, 0.0), f)
        for s in range(2):
            near, far = (0, 1) if s == 0 else (7, 6)
            for i in range(2):
                gs[s, pl.ds(2 * i * ROWS, ROWS)] = gx[i, col(near)]
                gs[s, pl.ds((2 * i + 1) * ROWS, ROWS)] = gx[i, col(far)]

        exchange_start((2, 3), answer_copy)

        for s in range(2):
            for i in range(7):
                ycf[s, i] = yf[i, col(7 * s)]

        for s in range(2):
            mid = sper[s, 0, pl.ds(1, ROWS)]
            fb = harmonic(sper[s, 0, pl.ds(0, ROWS)], mid)
            fa = harmonic(mid, sper[s, 0, pl.ds(2, ROWS)])
            fx = harmonic(mid, sper[s, 1, pl.ds(1, ROWS)])
            fo = harmonic(mid, perm[col(7 * s, ROWS, 1)])
            ff = harmonic(jnp.where(lane2 == 0, 0.0, roll_y(mid, 1)), mid)
            fk = harmonic(mid, jnp.where(lane2 == LANES - 1, 0.0, roll_y(mid, -1)))
            inv = active(row2) / (STORE + fb + fa + fx + fo + ff + fk)
            fb = jnp.where(row2 == 0, 0.0, fb * inv)
            fa = jnp.where(row2 == ROWS - 1, 0.0, fa * inv)
            ff, fk = ff * inv, fk * inv
            for i, f in enumerate((fb, fa, fx * inv, fo * inv, ff, fk)):
                sco[s, i] = f
            fy = reduce_factors(
                jnp.where(lane2 % BL == 0, 0.0, ff), jnp.where(lane2 % BL == BL - 1, 0.0, fk), roll_y
            )
            for i, f in enumerate(fy):
                syf[s, i] = f

    def update(t, e, at, scale=None):
        here = pl.ds(at, PIECE)
        v = e[pl.ds(at + 8, PIECE)]
        u = t[here] - (v if scale is None else v * scale)
        u = u + co[0, here] * e[here] + co[1, here] * e[pl.ds(at + 16, PIECE)]
        u = u + co[2, here] * roll_x(v, 1) + co[3, here] * roll_x(v, -1)
        return v, u + co[4, here] * roll_y(v, 1) + co[5, here] * roll_y(v, -1)

    def col_copy(ph, rows):
        def make(d, slot):
            return remote(
                d, cs.at[ph, d - 2, pl.ds(0, rows)], cr.at[ph, slot - 2, pl.ds(0, rows)],
                c_send.at[ph, d - 2], c_recv.at[ph, slot - 2],
            )
        return make

    def solved_copy(ph):
        def make(d, slot):
            if d < 4:
                return remote(
                    d, outs.at[ph, d - 2], outr.at[ph, slot - 2],
                    a_send.at[ph, d - 2], a_recv.at[ph, slot - 2],
                )
            return remote(
                d, outs.at[ph, d - 8], c2r.at[ph, slot - 8],
                c2_send.at[ph, d - 8], c2_recv.at[ph, slot - 8],
            )
        return make

    def one_round(outer, k):
        first = isinstance(k, int)
        ph = outer * ROUNDS + k
        om = relax_weight(0)
        if not first:
            for i in range(1, ROUNDS):
                om = jnp.where(k == i, jnp.float32(relax_weight(i)), om)
        for at in range(0, ROWS * 8, PIECE):
            here = pl.ds(at, PIECE)
            if first:
                e1[pl.ds(at + 8, PIECE)] = om * reduce_x(tgt[here], xfac(here))
            else:
                v, u = update(tgt, e0, at)
                e1[pl.ds(at + 8, PIECE)] = v + om * reduce_x(u, xfac(here))
        for s in range(2):
            near, far = (0, 1) if s == 0 else (7, 6)
            cs[ph, s, pl.ds(0, ROWS)] = e1[col(near, ROWS, 1)]
            cs[ph, s, pl.ds(ROWS, ROWS)] = e1[col(far, ROWS, 1)]
            if first:
                cs[ph, s, pl.ds(2 * ROWS, ROWS)] = tgt[col(near)]
        make = col_copy(ph, (3 if first else 2) * ROWS)
        exchange_start((2, 3), make)
        if first and outer == 0:
            rest_of_setup()
        if not first:
            exchange_wait((2, 3), solved_copy(ph))
            for z in range(ROWS):
                at, here = pl.ds((z + 1) * 8, 8), pl.ds(z * 8, 8)
                left = jnp.broadcast_to(outr[ph, 0, pl.ds(z, 1)], (8, LANES))
                right = jnp.broadcast_to(outr[ph, 1, pl.ds(z, 1)], (8, LANES))
                e1[at] = e1[at] + om * (gx[0, here] * left + gx[1, here] * right)
        for at in range(0, ROWS * 8, PIECE):
            here = pl.ds(at, PIECE)
            v, u = update(tgt, e1, at)
            e2[pl.ds(at + 8, PIECE)] = v + om * reduce_y(u, [yf[i, here] for i in range(7)])
        exchange_wait((2, 3), make)
        if not first:
            exchange_wait((8, 9), solved_copy(ph))
        for s in range(2):
            near, far = cr[ph, s, pl.ds(0, ROWS)], cr[ph, s, pl.ds(ROWS, ROWS)]
            if first:
                tside[s] = cr[ph, s, pl.ds(2 * ROWS, ROWS)]
            else:
                beyond, inner = c2r[ph, s], e0[col(7 * s, ROWS, 1)]
                left, right = (beyond, inner) if s == 0 else (inner, beyond)
                g = [gr[s, pl.ds(i * ROWS, ROWS)] for i in range(4)]
                near = near + om * (g[0] * left + g[2] * right)
                far = far + om * (g[1] * left + g[3] * right)
            u = tside[s] - near
            u = u + sco[s, 0] * roll_z(near, 1) + sco[s, 1] * roll_z(near, -1)
            u = u + sco[s, 2] * far + sco[s, 3] * e1[col(7 * s, ROWS, 1)]
            u = u + sco[s, 4] * roll_y(near, 1) + sco[s, 5] * roll_y(near, -1)
            beside = near + om * reduce_y(u, [syf[s, i] for i in range(7)])
            ub[col(7 * s)] = cx[s] * beside
            at = col(7 * s, ROWS, 1)
            e2[at] = e2[at] + om * reduce_y(cx[s] * near, [ycf[s, i] for i in range(7)])
        for at in range(0, ROWS * 8, PIECE):
            v, u = update(tgt, e2, at)
            u = (u + ub[pl.ds(at, PIECE)]).reshape(PIECE // CH, BL, 8, LANES)
            m, iv, up = (zf[i, pl.ds(at, PIECE)].reshape(u.shape) for i in range(3))
            v = v.reshape(u.shape)
            fw = [u[:, 0]]
            for i in range(1, BL):
                fw.append(u[:, i] - m[:, i] * fw[-1])
            nxt = None
            for i in range(BL - 1, -1, -1):
                x = fw[i] * iv[:, i]
                nxt = x if nxt is None else x - up[:, i] * nxt
                new = v[:, i] + om * nxt
                for c in range(PIECE // CH):
                    e0[pl.ds(at + c * CH + (i + 1) * 8, 8)] = new[c]

        def send_next():
            for s in range(2):
                outs[ph + 1, s] = e0[col(7 * s, ROWS, 1)]
            exchange_start((2, 3, 8, 9), solved_copy(ph + 1))

        if first:
            send_next()
        else:
            pl.when(k < ROUNDS - 1)(send_next)

    def mid_copy(d, slot):
        if d < 2:
            a, b = corr.at[pl.ds(0 if d == 0 else 120, 72)], mzr.at[slot]
        elif d < 4:
            a, b = mx.at[d - 2], mxr.at[slot - 2]
        else:
            z, s = divmod(d - 4, 2)
            a, b = mx.at[s, pl.ds(16 * z, 8)], mdr.at[slot - 4]
        return remote(d, a, b, m_send.at[d], m_recv.at[slot])

    def end_copy(d, slot):
        a = corr.at[pl.ds(0 if d == 0 else 160, 32)]
        return remote(d, a, fzr.at[slot], f_send.at[d], f_recv.at[slot])

    for outer in range(OUTER):
        for s in range(2):
            ub[col(7 * s)] = cx[s] * spre[s]
        for c in range(0, CHUNKS, PIECE // CH):
            rows = [active(rows_of(i)) for i in range(c, c + PIECE // CH)]
            here = pl.ds(c * CH, PIECE)
            tgt[here] = update(isrc, pres, c * CH, jnp.concatenate(rows))[1] + ub[here]
        one_round(outer, 0)
        if outer == 0:
            exchange_wait((2, 3), answer_copy)

        def step(k, carry, outer=outer):
            one_round(outer, k)
            return carry

        lax.fori_loop(1, ROUNDS, step, 0)
        if outer == 1:
            exchange_sent(range(8), [mid_copy])
        for c in range(CHUNKS):
            rows = rows_of(c)
            band = (rows < OV + low) | (rows >= OV + OWN - high)
            w = active(rows) * jnp.where(band, 0.5, 1.0)
            corr[pl.ds(c * CH, CH)] = w * e0[pl.ds((c * 8 + 1) * 8, CH)]
        if outer == 0:
            for s in range(2):
                mx[s] = corr[col(7 * s)]
            exchange_start(range(8), mid_copy)
            pres[pl.ds(8, ROWS * 8)] = pres[pl.ds(8, ROWS * 8)] + corr[...]
            exchange_wait(range(8), mid_copy)
            for z in range(2):
                at = pl.ds(0 if z == 0 else 17 * 8, 72)
                pres[at] = pres[at] + mzr[z]
            for s in range(2):
                spre[s] = spre[s] + mxr[s]
                for z in range(2):
                    at = pl.ds(16 * z, 8)
                    spre[s, at] = spre[s, at] + mdr[2 * z + s]
        else:
            exchange_start((0, 1), end_copy)
            later = [k for k in range(OUTER * ROUNDS) if k % ROUNDS]
            exchange_sent(range(8), [init_copy(0), init_copy(1)])
            makes = [col_copy(k, (2 if k % ROUNDS else 3) * ROWS) for k in range(OUTER * ROUNDS)]
            makes += [solved_copy(k) for k in later]
            exchange_sent((2, 3), makes + [answer_copy])
            exchange_sent((8, 9), [solved_copy(k) for k in later])
            exchange_sent((0, 1), [end_copy])
            pres[pl.ds(8, ROWS * 8)] = pres[pl.ds(8, ROWS * 8)] + corr[...]
            exchange_wait((0, 1), end_copy)
            for z in range(2):
                at = pl.ds(40 if z == 0 else 17 * 8, 32)
                pres[at] = pres[at] + fzr[z]
    out[...] = pres[pl.ds(40, OWN * 8)].reshape(OWN, 8, LANES)


def on_device(facies, facies_perm, perm_scale, source, pressure_start, intersection_depth):
    assert source.shape == (OWN, 8, LANES)
    f32 = jnp.float32

    def buf(*shape):
        return pltpu.VMEM(shape, f32)

    field, wide = (ROWS * 8, LANES), (WIDE * 8, LANES)
    phases, own, dma = OUTER * ROUNDS, source.shape, pltpu.SemaphoreType.DMA
    scratch = [
        pltpu.VMEM(own, jnp.int32), buf(*own), buf(*own), buf(*own),
        pltpu.SMEM(facies_perm.shape, f32), pltpu.SMEM(intersection_depth.shape, jnp.int32),
        dma((6,)), buf(2, 4 * ROWS, LANES), buf(2, 4 * ROWS, LANES),
        *[buf(phases, 2, ROWS, LANES)] * 3, buf(2, 7, ROWS, LANES),
        buf(2, 112, LANES), buf(2, 48, LANES), buf(4, 24, LANES),
        buf(2, 112, LANES), buf(2, 48, LANES), buf(4, 24, LANES),
        buf(2, ROWS, LANES), buf(2, 72, LANES), buf(2, ROWS, LANES), buf(4, 8, LANES),
        buf(2, 32, LANES), buf(phases, 2, 3 * ROWS, LANES), buf(phases, 2, 3 * ROWS, LANES),
        buf(*wide), buf(*wide), buf(2, 2, 32, LANES), buf(2, ROWS, LANES),
        buf(*field), buf(*field), buf(2, ROWS, LANES),
        buf(*wide), buf(*wide), buf(*wide), buf(*field), buf(*field),
        buf(6, *field), buf(4, *field), buf(7, *field), buf(3, *field),
        buf(2, *field), buf(2, ROWS, LANES), buf(2, 6, ROWS, LANES), buf(2, 7, ROWS, LANES),
    ]
    sems = [dma((2, 8)), dma((2, 8))] + [dma((n,)) for n in (8, 8, 2, 2, 2, 2)]
    sems += [dma((phases, 2)) for _ in range(6)]
    return pl.pallas_call(
        kernel,
        out_shape=jax.ShapeDtypeStruct(source.shape, f32),
        in_specs=[pl.BlockSpec(memory_space=pltpu.HBM)] * 6,
        out_specs=pl.BlockSpec(memory_space=pltpu.VMEM),
        scratch_shapes=scratch + sems,
        compiler_params=pltpu.CompilerParams(
            collective_id=0, has_side_effects=True, vmem_limit_bytes=60 * 1024 * 1024
        ),
        name="schwarz",
    )(facies, facies_perm, perm_scale, source, pressure_start, intersection_depth)


def solution(mesh):
    return jax.shard_map(
        on_device,
        mesh=mesh,
        in_specs=(
            P("sub", "grp", None),
            P(),
            P("sub", "grp", None),
            P("sub", "grp", None),
            P("sub", "grp", None),
            P(),
        ),
        out_specs=P("sub", "grp", None),
        check_vma=False,
    )
```
